32 devices in a mesh: ens: 2 (over x), lon: 8 (over z, y), lat: 2 (over core).
Axes of the slice: x: 2, y: 2, z: 4, core: 2. Of those that a mesh axis runs over, the one named last changes fastest.
Arguments:
- stream: float32 [6, 4, 24, 96, 512], P('ens', None, 'lat', 'lon'), parts along dimension 0, may hold values from -6 to 6
- region_ids: int32 [8, 24, 96], P('ens', 'lat', 'lon'), parts along dimension 0, may hold values from 0 to 2, as said below
- qkv_weight: bfloat16 [2, 512, 1536], replicated, may hold values from -0.25 to 0.25
- out_weight: bfloat16 [2, 512, 512], replicated, may hold values from -0.25 to 0.25
- up_weight: bfloat16 [2, 512, 2048], replicated, may hold values from -0.25 to 0.25
- down_weight: bfloat16 [2, 2048, 512], replicated, may hold values from -0.125 to 0.125
- norm_gain: float32 [2, 2, 512], replicated, may hold values from 0.5 to 1.5
- norm_bias: float32 [2, 2, 512], replicated, may hold values from -2 to 2
- logit_scale: float32 [2, 8], replicated, may hold values from 2 to 12
Outputs:
- mixed: float32 [6, 4, 24, 96, 512], P('ens', None, 'lat', 'lon'), parts along dimension 0
The draws below stay inside these ranges and needn't reach their ends.
There are 2 independent parts, one for each index of `ens`. The reference program is written for one: setup_inputs(seed, part) draws one part's arguments, and reference() takes and returns one part's arrays. A program takes and returns all parts, laid end to end along the dimension named above; an argument that names none is the same for every part. Nothing has to cross between parts.
Inputs may be any that keep to these rules, and one draw needn't show every extreme that they name: `region_ids`: within each window of the rolled frame the ids depend only on the longitude column: they are 0, 1, 2 in three contiguous runs of columns, each run one column or more, the same over all levels and latitude rows of the window.
All inputs are finite; a program needn't handle non-finite values.
Results may differ from the reference program's by a relative error of at most 0.008.
Values may be sent and summed in bfloat16 or wider, within the bound.
No kernel may reach another device: no remote copies, remote signals or barrier semaphores. Data moves between devices by JAX's collectives and lax.ppermute only.
A program may use at most 128 MiB of HBM per device.

```python
import math
import jax
import jax.numpy as jnp
from jax import lax

D = 512
HEADS = 8
FF = 2048
SAMPLES = 3
LEVELS = 4
WIN_LAT = 6
WIN_LON = 12
LAT = 24
LON = 96


def draw_region_ids(key, part):
    lat_blocks = LAT // WIN_LAT
    lon_blocks = LON // WIN_LON
    first_key, second_key = jax.random.split(jax.random.fold_in(key, 11))
    first_cut = jax.random.randint(first_key, (lat_blocks, lon_blocks), 1, WIN_LON // 2 + 1)
    second_cut = jax.random.randint(second_key, (lat_blocks, lon_blocks), WIN_LON // 2 + 1, WIN_LON)
    inside = jnp.arange(WIN_LON, dtype=jnp.int32)
    ids = (inside[None, None, :] >= first_cut[..., None]).astype(jnp.int32) + (inside[None, None, :] >= second_cut[..., None]).astype(jnp.int32)
    grid = jnp.broadcast_to(ids[:, None, :, :], (lat_blocks, WIN_LAT, lon_blocks, WIN_LON)).reshape(LAT, LON)
    return jnp.broadcast_to(grid[None], (LEVELS, LAT, LON)).astype(jnp.int32)


def block_scale(key, shape, pieces, least, high):
    level = 1.0
    for axis_at, shards_of in pieces:
        draws = jax.random.uniform(jax.random.fold_in(jax.random.fold_in(key, 6), axis_at), (shards_of,), jnp.float32, least / len(pieces), high / len(pieces))
        level = level * jnp.repeat(jnp.exp(draws), shape[axis_at] // shards_of).reshape((-1,) + (1,) * (len(shape) - 1 - axis_at))
    return level


def scatter_about(stream_key, extent, scale, limit, pieces=(), kind=jnp.bfloat16):
    values = jax.random.normal(stream_key, extent, jnp.float32) * scale
    if len(pieces) > 0:
        values = block_scale(stream_key, extent, pieces, -0.22, 0.18) * values
    return jnp.clip(values, min=-limit, max=limit).astype(kind)


def setup_inputs(seed: int = 0, part: int = 0) -> dict:
    seeds = jax.random.split(jax.random.key(seed), 10)
    own_keys = jax.random.split(jax.random.fold_in(seeds[9], part), 10)
    return {
        "stream": scatter_about(own_keys[0], (SAMPLES, LEVELS, LAT, LON, D), 1.0, 6.0, ((2, 2), (3, 8)), jnp.float32),
        "region_ids": draw_region_ids(jax.random.fold_in(jax.random.fold_in(seeds[9], part), 71), part),
        "qkv_weight": scatter_about(seeds[2], (2, D, 3 * D), D ** -0.5, 0.25),
        "out_weight": scatter_about(seeds[3], (2, D, D), D ** -0.5, 0.25),
        "up_weight": scatter_about(seeds[4], (2, D, FF), D ** -0.5, 0.25),
        "down_weight": scatter_about(seeds[5], (2, FF, D), FF ** -0.5, 0.125),
        "norm_gain": jnp.clip(1.0 + 0.1 * jax.random.normal(seeds[6], (2, 2, D), jnp.float32), 0.5, 1.5),
        "norm_bias": scatter_about(seeds[7], (2, 2, D), 0.3, 2.0, (), jnp.float32),
        "logit_scale": jnp.clip(jnp.exp(jax.random.uniform(seeds[8], (2, HEADS), jnp.float32, math.log(2.0), math.log(12.0))), 2.0, 12.0),
    }


highest = lax.Precision.HIGHEST

def norm_rows(values, gain_row, bias_row):
    average = lax.optimization_barrier(jnp.mean(values, -1, keepdims=True))
    centred = values - average
    spread = lax.optimization_barrier(jnp.mean(centred * centred, -1, keepdims=True))
    return centred / jnp.sqrt(spread + 1e-05) * gain_row + bias_row

def to_windows(grid):
    sample_count, level_count, lat_rows, lon_cols, channels = grid.shape
    blocks = grid.reshape(sample_count, level_count, lat_rows // WIN_LAT, WIN_LAT, lon_cols // WIN_LON, WIN_LON, channels)
    blocks = blocks.transpose(0, 2, 4, 1, 3, 5, 6)
    return blocks.reshape(-1, level_count * WIN_LAT * WIN_LON, channels)

def from_windows(blocks, sample_count, level_count, lat_rows, lon_cols):
    channels = blocks.shape[-1]
    grid = blocks.reshape(sample_count, lat_rows // WIN_LAT, lon_cols // WIN_LON, level_count, WIN_LAT, WIN_LON, channels)
    grid = grid.transpose(0, 3, 1, 4, 2, 5, 6)
    return grid.reshape(sample_count, level_count, lat_rows, lon_cols, channels)

def attend(triple, region_key, scale_row, head_count):
    win_tokens, three_width = triple.shape
    width = three_width // 3
    head_dim = width // head_count
    parts = triple.reshape(win_tokens, 3, head_count, head_dim).astype(jnp.float32)
    query = parts[:, 0]
    key_part = parts[:, 1]
    values = parts[:, 2]
    query_unit = query / jnp.sqrt(lax.optimization_barrier(jnp.sum(query * query, -1, keepdims=True)) + 1e-06)
    key_unit = key_part / jnp.sqrt(lax.optimization_barrier(jnp.sum(key_part * key_part, -1, keepdims=True)) + 1e-06)
    scores = jnp.einsum('ihd,jhd->hij', query_unit, key_unit, precision=highest)
    scores = scores * scale_row[:, None, None]
    weights = jnp.exp(scores)
    if region_key is not None:
        allowed = region_key[:, None] == region_key[None, :]
        weights = jnp.where(allowed[None], weights, jnp.zeros_like(weights))
    shares = (weights / lax.optimization_barrier(jnp.sum(weights, -1, keepdims=True))).astype(jnp.bfloat16)
    result = jnp.einsum('hij,jhd->ihd', shares.astype(jnp.float32), values, precision=highest)
    return result.reshape(win_tokens, width).astype(jnp.bfloat16)

def swin_layer(stream, layer_index, region_key, qkv_weight, out_weight, up_weight, down_weight, norm_gain, norm_bias, logit_scale):
    sample_count, level_count, lat_rows, lon_cols, width = stream.shape
    operand = stream.astype(jnp.bfloat16)
    if region_key is not None:
        operand = jnp.roll(operand, (-(WIN_LAT // 2), -(WIN_LON // 2)), axis=(2, 3))
    triple = jnp.dot(operand.reshape(-1, width), qkv_weight[layer_index], preferred_element_type=jnp.float32)
    triple = triple.astype(jnp.bfloat16).reshape(sample_count, level_count, lat_rows, lon_cols, 3 * width)
    blocks = to_windows(triple)
    scale_row = logit_scale[layer_index]
    head_count = scale_row.shape[0]
    if region_key is not None:
        full_key = jnp.broadcast_to(region_key[None], (sample_count,) + region_key.shape)
        key_blocks = to_windows(full_key[..., None])[..., 0]

        def masked_group(pair):
            return attend(pair[0], pair[1], scale_row, head_count)
        result = lax.map(masked_group, (blocks, key_blocks))
    else:

        def plain_group(group):
            return attend(group, None, scale_row, head_count)
        result = lax.map(plain_group, blocks)
    attended = from_windows(result, sample_count, level_count, lat_rows, lon_cols)
    if region_key is not None:
        attended = jnp.roll(attended, (WIN_LAT // 2, WIN_LON // 2), axis=(2, 3))
    projected = jnp.dot(attended.reshape(-1, width), out_weight[layer_index], preferred_element_type=jnp.float32)
    after = stream.reshape(-1, width) + norm_rows(projected, norm_gain[layer_index, 0], norm_bias[layer_index, 0])
    hidden = jax.nn.gelu(jnp.dot(after.astype(jnp.bfloat16), up_weight[layer_index], preferred_element_type=jnp.float32))
    hidden = hidden.astype(jnp.bfloat16)
    mlp_out = jnp.dot(hidden, down_weight[layer_index], preferred_element_type=jnp.float32)
    after = after + norm_rows(mlp_out, norm_gain[layer_index, 1], norm_bias[layer_index, 1])
    return after.reshape(sample_count, level_count, lat_rows, lon_cols, width)

def reference(stream, region_ids, qkv_weight, out_weight, up_weight, down_weight, norm_gain, norm_bias, logit_scale):
    lat_rows = stream.shape[2]
    position = jnp.arange(lat_rows, dtype=jnp.int32)
    band = (position >= lat_rows - WIN_LAT).astype(jnp.int32) + (position >= lat_rows - WIN_LAT // 2).astype(jnp.int32)
    region_key = region_ids * 3 + band[None, :, None]
    first = swin_layer(stream, 0, None, qkv_weight, out_weight, up_weight, down_weight, norm_gain, norm_bias, logit_scale)
    return swin_layer(first, 1, region_key, qkv_weight, out_weight, up_weight, down_weight, norm_gain, norm_bias, logit_scale)
```

```python
import functools

import jax
import jax.numpy as jnp
from jax import lax
from jax.experimental import pallas as pl
from jax.experimental.pallas import tpu as pltpu
from jax.sharding import PartitionSpec as P

WIN_LAT = 6
WIN_LON = 12
CELL_LAT = WIN_LAT // 2
CELL_LON = WIN_LON // 2
LOG2E = 1.4426950408889634
GELU_A = 0.7978845608028654
GELU_B = GELU_A * 0.044715
F32 = jnp.float32
BF16 = jnp.bfloat16
VMEM_LIMIT = 56 * 1024 * 1024


def dot(a, b):
    return jnp.dot(a, b, preferred_element_type=F32)


def dot_t(a, b):
    return lax.dot_general(a, b, (((1,), (1,)), ((), ())), preferred_element_type=F32)


def norm_rows(values, gain_row, bias_row):
    average = jnp.mean(values, -1, keepdims=True)
    centred = values - average
    spread = jnp.mean(centred * centred, -1, keepdims=True)
    return centred * lax.rsqrt(spread + 1e-05) * gain_row + bias_row


def lane_head(rows, lanes, head_dim):
    return lax.broadcasted_iota(jnp.int32, (rows, lanes), 1) // head_dim


def scale_lanes(scale_ref, layer, width, heads):
    head_of = lane_head(1, width, width // heads)
    row = jnp.zeros((1, width), F32)
    for h in range(heads):
        row = jnp.where(head_of == h, scale_ref[layer, h] * LOG2E, row)
    return row


def attend(triple, scale_row, same, heads):
    tokens, width = triple.shape[0], triple.shape[1] // 3
    head_dim = width // heads
    group = 256
    in_group = group // head_dim
    pair_lanes = 2 * head_dim
    keys = in_group * tokens
    spare = -(2 * tokens) % 128
    ones_block = (
        lax.broadcasted_iota(jnp.int32, (group, group), 0) // head_dim
        == lane_head(group, group, head_dim)
    ).astype(BF16)
    head_of = lane_head(1, group, head_dim)
    pieces = []
    for g in range(width // group):
        at = g * group
        q = triple[:, at : at + group]
        k = triple[:, width + at : width + at + group]
        v = triple[:, 2 * width + at : 2 * width + at + group].astype(BF16)
        qn = q * (lax.rsqrt(dot((q * q).astype(BF16), ones_block) + 1e-06) * scale_row[:, at : at + group])
        kn = k * lax.rsqrt(dot((k * k).astype(BF16), ones_block) + 1e-06)
        qn = qn.astype(BF16)
        kn = kn.astype(BF16)
        k_block = jnp.concatenate(
            [kn * (head_of == h).astype(BF16) for h in range(in_group)], axis=0
        )
        weights = jnp.exp2(dot_t(qn, k_block))
        if same is not None:
            weights = weights * same
        weights = weights.astype(BF16)
        for p in range(in_group // 2):
            vp = v[:, p * pair_lanes : (p + 1) * pair_lanes]
            low = (lane_head(1, pair_lanes, head_dim) == 0).astype(BF16)
            high = (lane_head(1, pair_lanes, head_dim) == 1).astype(BF16)
            one = jnp.ones((tokens, pair_lanes), BF16)
            rows = jnp.concatenate(
                [
                    jnp.concatenate([vp * low, one * low], axis=1),
                    jnp.concatenate([vp * high, one * high], axis=1),
                ],
                axis=0,
            )
            first = p * 2 * tokens
            start = first // 128 * 128
            stop = min(keys, -(-(first + 2 * tokens) // 128) * 128)
            parts = []
            if first > start:
                parts.append(jnp.zeros((first - start, 2 * pair_lanes), BF16))
            parts.append(rows)
            if stop > first + 2 * tokens:
                parts.append(jnp.zeros((stop - first - 2 * tokens, 2 * pair_lanes), BF16))
            rows = jnp.concatenate(parts, axis=0)
            both = dot(weights[:, start:stop], rows)
            pieces.append((both[:, :pair_lanes] / both[:, pair_lanes:]).astype(BF16))
    return jnp.concatenate(pieces, axis=1)


def feed_forward(after, up_ref, down_ref, chunk):
    after_b = after.astype(BF16)
    hidden_width = up_ref.shape[1]
    total = None
    for at in range(0, hidden_width, chunk):
        u = dot(after_b, up_ref[:, at : at + chunk])
        half = 0.5 * u
        h = half + half * jnp.tanh(u * (GELU_A + GELU_B * (u * u)))
        part = dot(h.astype(BF16), down_ref[at : at + chunk, :])
        total = part if total is None else total + part
    return total


def finish_rows(x, attended, out_ref, up_ref, down_ref, gain_ref, bias_ref, layer):
    after = x + norm_rows(dot(attended, out_ref[...]), gain_ref[layer, 0:1], bias_ref[layer, 0:1])
    mlp = feed_forward(after, up_ref, down_ref, 512)
    return after + norm_rows(mlp, gain_ref[layer, 1:2], bias_ref[layer, 1:2])


def weight_copies(layer, pairs, sems):
    return [
        pltpu.make_async_copy(src.at[layer], dst, sems.at[n]) for n, (src, dst) in enumerate(pairs)
    ]


def first_kernel(
    heads, levels,
    x_ref, scale_ref, gain_ref, bias_ref, qkv_hbm, out_hbm, up_hbm, down_hbm,
    first_ref, east_ref, west_ref, east0_ref, west0_ref,
    x_s, qkv_s, out_s, up_s, down_s, sems,
):
    i = pl.program_id(0)
    width = x_ref.shape[-1]
    cell = levels * CELL_LAT * CELL_LON
    copies = weight_copies(
        0, [(qkv_hbm, qkv_s), (out_hbm, out_s), (up_hbm, up_s), (down_hbm, down_s)], sems
    )

    @pl.when(i == 0)
    def _():
        for c in copies:
            c.start()

    for half in range(2):
        for r in range(WIN_LAT):
            for l in range(levels):
                row = (half * 2 + r // CELL_LAT) * cell + (l * CELL_LAT + r % CELL_LAT) * CELL_LON
                x_s[row : row + CELL_LON, :] = x_ref[0, l, r, half * CELL_LON : (half + 1) * CELL_LON, :]

    @pl.when(i == 0)
    def _():
        copies[0].wait()

    x = x_s[...]
    triple = dot(x.astype(BF16), qkv_s[...])
    attended = attend(triple, scale_lanes(scale_ref, 0, width, heads), None, heads)

    @pl.when(i == 0)
    def _():
        for c in copies[1:]:
            c.wait()

    first = finish_rows(x, attended, out_s, up_s, down_s, gain_ref, bias_ref, 0)
    for half in range(2):
        for r in range(2):
            rows = first[(half * 2 + r) * cell : (half * 2 + r + 1) * cell]
            first_ref[half, r] = rows
            kept, kept0 = (west_ref, west0_ref) if half == 0 else (east_ref, east0_ref)
            if r == 0:

                @pl.when(i == 0)
                def _():
                    kept0[...] = rows.astype(BF16)

                @pl.when(i > 0)
                def _():
                    kept[2 * i - 1] = rows.astype(BF16)

            else:
                kept[2 * i] = rows.astype(BF16)


def shifted_kernel(
    heads,
    east_ref, west_ref, east0_ref, west0_ref, codes_ref, scale_ref, qkv_hbm,
    to_east_ref, to_west_ref, to_east0_ref, to_west0_ref,
    x_s, att_s, qkv_s, sems,
):
    windows, tokens, width = x_s.shape
    cell = tokens // 4
    copies = weight_copies(1, [(qkv_hbm, qkv_s)], sems)
    copies[0].start()

    def cells(i, e, w, e0, w0):
        last = i == windows - 1
        return [
            e.at[2 * i],
            e0 if last else e.at[2 * i + 1],
            w.at[2 * i],
            w0 if last else w.at[2 * i + 1],
        ]

    for i in range(windows):
        for n, ref in enumerate(cells(i, east_ref, west_ref, east0_ref, west0_ref)):
            x_s[i, n * cell : (n + 1) * cell, :] = ref[...].astype(F32)
    copies[0].wait()
    scale_row = scale_lanes(scale_ref, 1, width, heads)

    @pl.loop(0, windows)
    def _(i):
        codes = codes_ref[i]
        same = dot_t(codes, jnp.concatenate([codes] * (256 * heads // width), axis=0))
        triple = dot(x_s[i].astype(BF16), qkv_s[...])
        att_s[i] = attend(triple, scale_row, same, heads).astype(F32)

    for i in range(windows):
        for n, ref in enumerate(cells(i, to_east_ref, to_west_ref, to_east0_ref, to_west0_ref)):
            ref[...] = att_s[i, n * cell : (n + 1) * cell, :].astype(BF16)


def last_kernel(
    levels, has_prior,
    first_ref, east_ref, west_ref, east0_ref, west0_ref, gain_ref, bias_ref, out_hbm, up_hbm, down_hbm,
    *rest,
):
    if has_prior:
        rest = rest[1:]
    mixed_ref, y_s, out_s, up_s, down_s, sems = rest
    i = pl.program_id(0)
    width = first_ref.shape[-1]
    cell = levels * CELL_LAT * CELL_LON
    copies = weight_copies(1, [(out_hbm, out_s), (up_hbm, up_s), (down_hbm, down_s)], sems)

    @pl.when(i == 0)
    def _():
        for c in copies:
            c.start()

    pieces = []
    for half in range(2):
        kept, kept0 = (west_ref, west0_ref) if half == 0 else (east_ref, east0_ref)
        before = kept[jnp.maximum(2 * i - 1, 0)].astype(F32)
        pieces.append(jnp.where(i == 0, kept0[...].astype(F32), before))
        pieces.append(kept[2 * i].astype(F32))
    attended = jnp.concatenate(pieces, axis=0).astype(BF16)
    x = jnp.concatenate([first_ref[h, r] for h in range(2) for r in range(2)], axis=0)

    @pl.when(i == 0)
    def _():
        for c in copies:
            c.wait()

    y_s[...] = finish_rows(x, attended, out_s, up_s, down_s, gain_ref, bias_ref, 1)
    for half in range(2):
        for r in range(WIN_LAT):
            for l in range(levels):
                row = (half * 2 + r // CELL_LAT) * cell + (l * CELL_LAT + r % CELL_LAT) * CELL_LON
                mixed_ref[0, l, r, half * CELL_LON : (half + 1) * CELL_LON, :] = y_s[row : row + CELL_LON, :]


def whole(shape):
    return pl.BlockSpec(shape, lambda *_: (0,) * len(shape))


ANY = pl.BlockSpec(memory_space=pl.ANY)
SMEM = pl.BlockSpec(memory_space=pltpu.SMEM)


def params():
    return pltpu.CompilerParams(vmem_limit_bytes=VMEM_LIMIT)


def first_layer(stream, sample, scale, gain, bias, qkv, out, up, down):
    _, levels, lat_rows, lon_cols, width = stream.shape
    windows = lat_rows // WIN_LAT
    bands = lat_rows // CELL_LAT
    cell = levels * CELL_LAT * CELL_LON
    heads = scale.shape[1]
    kept = jax.ShapeDtypeStruct((bands - 1, cell, width), BF16)
    kept0 = jax.ShapeDtypeStruct((cell, width), BF16)
    tokens = 4 * cell
    return pl.pallas_call(
        functools.partial(first_kernel, heads, levels),
        grid=(windows,),
        in_specs=[
            pl.BlockSpec((1, levels, WIN_LAT, lon_cols, width), lambda i: (sample, 0, i, 0, 0)),
            SMEM, whole(gain.shape), whole(bias.shape), ANY, ANY, ANY, ANY,
        ],
        out_specs=[
            pl.BlockSpec((2, 2, cell, width), lambda i: (0, i, 0, 0)),
            whole(kept.shape), whole(kept.shape), whole(kept0.shape), whole(kept0.shape),
        ],
        out_shape=[
            jax.ShapeDtypeStruct((2, bands, cell, width), F32), kept, kept, kept0, kept0,
        ],
        scratch_shapes=[
            pltpu.VMEM((tokens, width), F32),
            pltpu.VMEM(qkv.shape[1:], BF16),
            pltpu.VMEM(out.shape[1:], BF16),
            pltpu.VMEM(up.shape[1:], BF16),
            pltpu.VMEM(down.shape[1:], BF16),
            pltpu.SemaphoreType.DMA((4,)),
        ],
        compiler_params=params(),
        cost_estimate=pl.CostEstimate(flops=8 * 10**9, bytes_accessed=10**7, transcendentals=0),
        name="first_layer",
    )(stream, scale, gain, bias, qkv, out, up, down)


def shifted_attention(east, west, east0, west0, codes, scale, qkv):
    windows, tokens, _ = codes.shape
    width = east.shape[-1]
    args = (east, west, east0, west0)
    return pl.pallas_call(
        functools.partial(shifted_kernel, scale.shape[1]),
        in_specs=[pl.BlockSpec(memory_space=pltpu.VMEM)] * 5 + [SMEM, ANY],
        out_specs=[pl.BlockSpec(memory_space=pltpu.VMEM)] * 4,
        out_shape=[jax.ShapeDtypeStruct(a.shape, BF16) for a in args],
        scratch_shapes=[
            pltpu.VMEM((windows, tokens, width), F32),
            pltpu.VMEM((windows, tokens, width), F32),
            pltpu.VMEM(qkv.shape[1:], BF16),
            pltpu.SemaphoreType.DMA((1,)),
        ],
        compiler_params=params(),
        cost_estimate=pl.CostEstimate(flops=4 * 10**9, bytes_accessed=5 * 10**6, transcendentals=0),
        name="shifted_attention",
    )(*args, codes, scale, qkv)


def last_half(first, east, west, east0, west0, sample, samples, lat_rows, levels, prior, gain, bias, out, up, down):
    width = first.shape[-1]
    windows = lat_rows // WIN_LAT
    cell = first.shape[2]
    shape = (samples, levels, lat_rows, WIN_LON, width)
    more = [] if prior is None else [prior]
    return pl.pallas_call(
        functools.partial(last_kernel, levels, prior is not None),
        grid=(windows,),
        in_specs=[
            pl.BlockSpec((2, 2, cell, width), lambda i: (0, i, 0, 0)),
            whole(east.shape), whole(west.shape), whole(east0.shape), whole(west0.shape),
            whole(gain.shape), whole(bias.shape), ANY, ANY, ANY,
        ] + [ANY] * len(more),
        out_specs=pl.BlockSpec((1, levels, WIN_LAT, WIN_LON, width), lambda i: (sample, 0, i, 0, 0)),
        out_shape=jax.ShapeDtypeStruct(shape, F32),
        scratch_shapes=[
            pltpu.VMEM((4 * cell, width), F32),
            pltpu.VMEM(out.shape[1:], BF16),
            pltpu.VMEM(up.shape[1:], BF16),
            pltpu.VMEM(down.shape[1:], BF16),
            pltpu.SemaphoreType.DMA((3,)),
        ],
        input_output_aliases={10: 0} if more else {},
        compiler_params=params(),
        cost_estimate=pl.CostEstimate(flops=5 * 10**9, bytes_accessed=10**7, transcendentals=0),
        name="last_half",
    )(first, east, west, east0, west0, gain, bias, out, up, down, *more)


def shifted(x, lat_by, lon_by):
    lat, lon = lax.axis_size("lat"), lax.axis_size("lon")
    pairs = [
        (o * lat + a, (o + lon_by) % lon * lat + (a + lat_by) % lat)
        for o in range(lon)
        for a in range(lat)
    ]
    return lax.ppermute(x, ("lon", "lat"), pairs)


def window_codes(region_ids, lat_rows):
    levels = region_ids.shape[0]
    windows = lat_rows // WIN_LAT
    lat_total = lax.axis_size("lat") * lat_rows
    lon_ids = region_ids[0, ::WIN_LAT, :].reshape(windows, 2, 1, 1, 1, CELL_LON)
    start = lax.axis_index("lat") * lat_rows + CELL_LAT * jnp.arange(2 * windows, dtype=jnp.int32)
    band = (start >= lat_total - WIN_LAT).astype(jnp.int32) + (
        start >= lat_total - CELL_LAT
    ).astype(jnp.int32)
    key = lon_ids * 3 + band.reshape(windows, 1, 2, 1, 1, 1)
    key = jnp.broadcast_to(key, (windows, 2, 2, levels, CELL_LAT, CELL_LON)).reshape(windows, -1)
    return (key[:, :, None] == jnp.arange(128, dtype=jnp.int32)).astype(BF16)


def local(stream, region_ids, qkv, out, up, down, gain, bias, scale):
    samples, levels, lat_rows, _, _ = stream.shape
    codes = window_codes(region_ids, lat_rows)
    firsts, halos = [], []
    for s in range(samples):
        first, east, west, east0, west0 = first_layer(stream, s, scale, gain, bias, qkv, out, up, down)
        firsts.append(first)
        halos.append((east, shifted(west, 0, -1), shifted(east0, -1, 0), shifted(west0, -1, -1)))
    backs = []
    for s in range(samples):
        east, west, east0, west0 = shifted_attention(*halos[s], codes, scale, qkv)
        backs.append((east, shifted(west, 0, 1), shifted(east0, 1, 0), shifted(west0, 1, 1)))
    mixed = None
    for s in range(samples):
        mixed = last_half(firsts[s], *backs[s], s, samples, lat_rows, levels, mixed, gain, bias, out, up, down)
    return mixed


def solution(mesh):
    in_specs = (
        P("ens", None, "lat", "lon", None),
        P("ens", "lat", "lon"),
        P(), P(), P(), P(), P(), P(), P(),
    )
    out_specs = P("ens", None, "lat", "lon", None)
    return jax.shard_map(local, mesh=mesh, in_specs=in_specs, out_specs=out_specs, check_vma=False)
```

```python
import functools

import jax
import jax.numpy as jnp
from jax import lax
from jax.experimental import pallas as pl
from jax.experimental.pallas import tpu as pltpu
from jax.sharding import PartitionSpec as P

WIN_LAT = 6
WIN_LON = 12
CELL_LAT = WIN_LAT // 2
CELL_LON = WIN_LON // 2
LOG2E = 1.4426950408889634
GELU_A = 0.7978845608028654
GELU_B = GELU_A * 0.044715
F32 = jnp.float32
BF16 = jnp.bfloat16


def dot(a, b):
    return jnp.dot(a, b, preferred_element_type=F32)


def dot_t(a, b):
    return lax.dot_general(a, b, (((1,), (1,)), ((), ())), preferred_element_type=F32)


def norm_rows(values, gain_row, bias_row):
    average = jnp.mean(values, -1, keepdims=True)
    centred = values - average
    spread = jnp.mean(centred * centred, -1, keepdims=True)
    return centred * lax.rsqrt(spread + 1e-05) * gain_row + bias_row


def lane_head(rows, lanes, head_dim):
    return lax.broadcasted_iota(jnp.int32, (rows, lanes), 1) // head_dim


def scale_lanes(scale_ref, layer, width, heads):
    head_of = lane_head(1, width, width // heads)
    row = jnp.zeros((1, width), F32)
    for h in range(heads):
        row = jnp.where(head_of == h, scale_ref[layer, h] * LOG2E, row)
    return row


def attend(triple, scale_row, same, heads):
    tokens, width = triple.shape[0], triple.shape[1] // 3
    head_dim = width // heads
    group = 256
    in_group = group // head_dim
    pair_lanes = 2 * head_dim
    keys = in_group * tokens
    spare = -(2 * tokens) % 128
    ones_block = (
        lax.broadcasted_iota(jnp.int32, (group, group), 0) // head_dim
        == lane_head(group, group, head_dim)
    ).astype(BF16)
    head_of = lane_head(1, group, head_dim)
    pieces = []
    for g in range(width // group):
        at = g * group
        q = triple[:, at : at + group]
        k = triple[:, width + at : width + at + group]
        v = triple[:, 2 * width + at : 2 * width + at + group]
        qn = (q * (lax.rsqrt(dot(q * q, ones_block) + 1e-06) * scale_row[:, at : at + group])).astype(BF16)
        kn = (k * lax.rsqrt(dot(k * k, ones_block) + 1e-06)).astype(BF16)
        k_block = jnp.concatenate(
            [kn * (head_of == h).astype(BF16) for h in range(in_group)], axis=0
        )
        weights = jnp.exp2(dot_t(qn, k_block)).astype(BF16)
        if same is not None:
            weights = weights * same
        for p in range(in_group // 2):
            vp = v[:, p * pair_lanes : (p + 1) * pair_lanes]
            low = (lane_head(1, pair_lanes, head_dim) == 0).astype(BF16)
            high = (lane_head(1, pair_lanes, head_dim) == 1).astype(BF16)
            one = jnp.ones((tokens, pair_lanes), BF16)
            rows = jnp.concatenate(
                [
                    jnp.concatenate([vp * low, one * low], axis=1),
                    jnp.concatenate([vp * high, one * high], axis=1),
                ],
                axis=0,
            )
            first = p * 2 * tokens
            start = first // 128 * 128
            stop = min(keys, -(-(first + 2 * tokens) // 128) * 128)
            parts = []
            if first > start:
                parts.append(jnp.zeros((first - start, 2 * pair_lanes), BF16))
            parts.append(rows)
            if stop > first + 2 * tokens:
                parts.append(jnp.zeros((stop - first - 2 * tokens, 2 * pair_lanes), BF16))
            rows = jnp.concatenate(parts, axis=0)
            both = dot(weights[:, start:stop], rows)
            pieces.append((both[:, :pair_lanes] / both[:, pair_lanes:]).astype(BF16))
    return jnp.concatenate(pieces, axis=1)


def gelu(u):
    u = u.astype(BF16)
    half = BF16(0.5) * u
    return half + half * jnp.tanh(u * (BF16(GELU_A) + BF16(GELU_B) * (u * u)))


def feed_forward(after, up_ref, down_ref, chunk):
    after_b = after.astype(BF16)
    hidden_width = up_ref.shape[1]
    total = None
    for at in range(0, hidden_width, chunk):
        h = gelu(dot(after_b, up_ref[:, at : at + chunk]))
        part = dot(h, down_ref[at : at + chunk, :])
        total = part if total is None else total + part
    return total


def finish_rows(x, attended, out_ref, up_ref, down_ref, gain_ref, bias_ref, layer):
    after = x + norm_rows(dot(attended, out_ref[...]), gain_ref[layer, 0:1], bias_ref[layer, 0:1])
    mlp = feed_forward(after, up_ref, down_ref, 1024)
    return after + norm_rows(mlp, gain_ref[layer, 1:2], bias_ref[layer, 1:2])


def first_kernel(
    heads, sample, load,
    grid_hbm, scale_ref, gain_ref, bias_ref, qkv_ref, out_ref, up_ref, down_ref,
    first_ref, east_ref, west_ref, east0_ref, west0_ref,
    x_ref, x_s, tri_s, att_s, x_sems, *held,
):
    rows, cols, levels, width = x_ref.shape
    parts = x_sems.shape[0]
    x_copies = [
        pltpu.make_async_copy(
            grid_hbm.at[sample, pl.ds(n * rows // parts, rows // parts)],
            x_ref.at[pl.ds(n * rows // parts, rows // parts)],
            x_sems.at[n],
        )
        for n in range(parts)
    ]
    for c in x_copies:
        c.start()
    weights = [qkv_ref, out_ref, up_ref, down_ref]
    copies = []
    if load:
        sems, held = held[0], held[1:]
        copies = [
            pltpu.make_async_copy(src.at[0], dst, sems.at[n])
            for n, (src, dst) in enumerate(zip(weights, held))
        ]
        for c in copies:
            c.start()
        qkv_ref, out_ref, up_ref, down_ref = held
    else:
        qkv_ref, out_ref, up_ref, down_ref = [w.at[0] for w in weights]
    for c in x_copies:
        c.wait()
    bands = rows // CELL_LAT
    windows = bands // 2
    line = CELL_LON * levels
    cell = CELL_LAT * line
    for half in range(2):
        for r in range(rows):
            x_s[half, r * line : (r + 1) * line, :] = x_ref[
                r, half * CELL_LON : (half + 1) * CELL_LON
            ].reshape(line, width)
    x = x_s[...].reshape(2 * bands * cell, width)
    for c in copies[:1]:
        c.wait()
    tri_s[...] = dot(x.astype(BF16), qkv_ref[...]).astype(BF16).reshape(tri_s.shape)
    scale_row = scale_lanes(scale_ref, 0, width, heads)
    for i in range(windows):
        part = slice(2 * cell * i, 2 * cell * (i + 1))
        triple = tri_s[:, part].reshape(4 * cell, 3 * width)
        att_s[:, part] = attend(triple, scale_row, None, heads).reshape(2, 2 * cell, width)
    attended = att_s[...].reshape(2 * bands * cell, width)
    for c in copies[1:]:
        c.wait()
    first = finish_rows(x, attended, out_ref, up_ref, down_ref, gain_ref, bias_ref, 0)
    for half in range(2):
        kept, kept0 = (west_ref, west0_ref) if half == 0 else (east_ref, east0_ref)
        for r in range(bands):
            part = first[(half * bands + r) * cell : (half * bands + r + 1) * cell]
            first_ref[half, r] = part
            if r == 0:
                kept0[...] = part.astype(BF16)
            else:
                kept[r - 1] = part.astype(BF16)


def shifted_kernel(
    heads,
    east_ref, west_ref, east0_ref, west0_ref, ids_ref, scale_ref, qkv_ref,
    to_east_ref, to_west_ref, to_east0_ref, to_west0_ref,
):
    cell, width = east0_ref.shape
    windows = ids_ref.shape[0] // WIN_LAT
    tokens = 4 * cell

    def cells(i, e, w, e0, w0):
        last = i == windows - 1
        return [
            e.at[2 * i],
            e0 if last else e.at[2 * i + 1],
            w.at[2 * i],
            w0 if last else w.at[2 * i + 1],
        ]

    x = jnp.concatenate(
        [
            ref[...].astype(F32)
            for i in range(windows)
            for ref in cells(i, east_ref, west_ref, east0_ref, west0_ref)
        ],
        axis=0,
    ).astype(BF16)
    triple = dot(x, qkv_ref[1]).astype(BF16)
    scale_row = scale_lanes(scale_ref, 1, width, heads)
    for i in range(windows):
        codes = window_codes(ids_ref, i, cell)
        same = dot_t(codes, jnp.concatenate([codes] * (256 * heads // width), axis=0)).astype(BF16)
        att = attend(triple[i * tokens : (i + 1) * tokens], scale_row, same, heads).astype(F32)
        for n, ref in enumerate(cells(i, to_east_ref, to_west_ref, to_east0_ref, to_west0_ref)):
            ref[...] = att[n * cell : (n + 1) * cell, :].astype(BF16)


def last_kernel(
    has_prior,
    first_ref, east_ref, west_ref, east0_ref, west0_ref, gain_ref, bias_ref, out_ref, up_ref, down_ref,
    *rest,
):
    mixed_ref = rest[1] if has_prior else rest[0]
    out_ref, up_ref, down_ref = out_ref.at[1], up_ref.at[1], down_ref.at[1]
    _, bands, cell, width = first_ref.shape
    line = cell // CELL_LAT
    pieces = []
    for half in range(2):
        kept, kept0 = (west_ref, west0_ref) if half == 0 else (east_ref, east0_ref)
        pieces.append(kept0[...].astype(F32))
        pieces.extend(kept[r].astype(F32) for r in range(bands - 1))
    attended = jnp.concatenate(pieces, axis=0).astype(BF16)
    x = first_ref[...].reshape(2 * bands * cell, width)
    y = finish_rows(x, attended, out_ref, up_ref, down_ref, gain_ref, bias_ref, 1)
    for half in range(2):
        for r in range(bands * CELL_LAT):
            at = half * bands * cell + r * line
            mixed_ref[0, r, half * CELL_LON : (half + 1) * CELL_LON] = y[at : at + line].reshape(
                CELL_LON, line // CELL_LON, width
            )


def whole(shape):
    return pl.BlockSpec(shape, lambda *_: (0,) * len(shape))


ANY = pl.BlockSpec(memory_space=pl.ANY)
HBM = pl.BlockSpec(memory_space=pltpu.HBM)
SMEM = pl.BlockSpec(memory_space=pltpu.SMEM)
VMEM = pl.BlockSpec(memory_space=pltpu.VMEM)


def params(limit):
    return pltpu.CompilerParams(vmem_limit_bytes=limit << 20)


def first_layer(grid, sample, scale, gain, bias, *weights):
    _, rows, cols, levels, width = grid.shape
    load = sample == 0
    bands = rows // CELL_LAT
    cell = levels * CELL_LAT * CELL_LON
    kept = jax.ShapeDtypeStruct((bands - 1, cell, width), BF16)
    kept0 = jax.ShapeDtypeStruct((cell, width), BF16)
    held = []
    grid = pltpu.with_memory_space_constraint(grid, pltpu.HBM)
    if load:
        weights = [pltpu.with_memory_space_constraint(w, pltpu.HBM) for w in weights]
        held = [pltpu.SemaphoreType.DMA((4,))] + [pltpu.VMEM(w.shape[1:], BF16) for w in weights]
    return pl.pallas_call(
        functools.partial(first_kernel, scale.shape[1], sample, load),
        in_specs=[HBM, SMEM, VMEM, VMEM] + [HBM if load else VMEM] * 4,
        out_specs=[VMEM] * 5,
        out_shape=[
            jax.ShapeDtypeStruct((2, bands, cell, width), F32), kept, kept, kept0, kept0,
        ],
        scratch_shapes=[
            pltpu.VMEM(grid.shape[1:], F32),
            pltpu.VMEM((2, bands * cell, width), F32),
            pltpu.VMEM((2, bands * cell, 3 * width), BF16),
            pltpu.VMEM((2, bands * cell, width), BF16),
            pltpu.SemaphoreType.DMA((2,)),
        ] + held,
        compiler_params=params(24 if load else 16),
        cost_estimate=pl.CostEstimate(flops=8 * 10**9, bytes_accessed=10**7, transcendentals=0),
        name="first_layer",
    )(grid, scale, gain, bias, *weights)


def shifted_attention(east, west, east0, west0, ids, scale, qkv):
    args = (east, west, east0, west0)
    return pl.pallas_call(
        functools.partial(shifted_kernel, scale.shape[1]),
        in_specs=[VMEM] * 4 + [SMEM, SMEM, VMEM],
        out_specs=[VMEM] * 4,
        out_shape=[jax.ShapeDtypeStruct(a.shape, BF16) for a in args],
        compiler_params=params(14),
        cost_estimate=pl.CostEstimate(flops=4 * 10**9, bytes_accessed=5 * 10**6, transcendentals=0),
        name="shifted_attention",
    )(*args, ids, scale, qkv)


def last_half(first, east, west, east0, west0, sample, shape, prior, gain, bias, out, up, down):
    more = [] if prior is None else [prior]
    return pl.pallas_call(
        functools.partial(last_kernel, prior is not None),
        grid=(1,),
        in_specs=[VMEM] * 10 + [ANY] * len(more),
        out_specs=pl.BlockSpec((1,) + shape[1:], lambda i: (sample, 0, 0, 0, 0)),
        out_shape=jax.ShapeDtypeStruct(shape, F32),
        input_output_aliases={10: 0} if more else {},
        compiler_params=params(14),
        cost_estimate=pl.CostEstimate(flops=5 * 10**9, bytes_accessed=10**7, transcendentals=0),
        name="last_half",
    )(first, east, west, east0, west0, gain, bias, out, up, down, *more)


def shifted(x, lat_by, lon_by):
    lat, lon = lax.axis_size("lat"), lax.axis_size("lon")
    pairs = [
        (o * lat + a, (o + lon_by) % lon * lat + (a + lat_by) % lat)
        for o in range(lon)
        for a in range(lat)
    ]
    return lax.ppermute(x, ("lon", "lat"), pairs)


def window_codes(ids_ref, window, cell):
    rows, levels, _ = ids_ref.shape
    lat_total = lax.axis_size("lat") * rows
    start = lax.axis_index("lat") * rows + window * WIN_LAT
    token = lax.broadcasted_iota(jnp.int32, (cell, 128), 0)
    column = lax.rem(token // levels, CELL_LON)
    lane = lax.broadcasted_iota(jnp.int32, (cell, 128), 1)
    codes = []
    for half in range(2):
        ids = jnp.zeros((cell, 128), jnp.int32)
        for c in range(CELL_LON):
            ids = jnp.where(column == c, ids_ref[window * WIN_LAT, 0, half * CELL_LON + c], ids)
        for r in range(2):
            at = start + r * CELL_LAT
            band = jnp.where(at >= lat_total - WIN_LAT, 1, 0) + jnp.where(
                at >= lat_total - CELL_LAT, 1, 0
            )
            codes.append(jnp.where(ids * 3 + band == lane, 1.0, 0.0))
    return jnp.concatenate(codes, axis=0).astype(BF16)


def local(stream, region_ids, qkv, out, up, down, gain, bias, scale):
    samples = stream.shape[0]
    ids = region_ids.transpose(1, 0, 2)
    grid = stream.transpose(0, 2, 3, 1, 4)
    firsts, halos = [], []
    for s in range(samples):
        first, east, west, east0, west0 = first_layer(grid, s, scale, gain, bias, qkv, out, up, down)
        firsts.append(first)
        halos.append((east, shifted(west, 0, -1), shifted(east0, -1, 0), shifted(west0, -1, -1)))
    backs = []
    for s in range(samples):
        east, west, east0, west0 = shifted_attention(*halos[s], ids, scale, qkv)
        backs.append((east, shifted(west, 0, 1), shifted(east0, 1, 0), shifted(west0, 1, 1)))
    mixed = None
    for s in range(samples):
        mixed = last_half(firsts[s], *backs[s], s, grid.shape, mixed, gain, bias, out, up, down)
    return mixed.transpose(0, 3, 1, 2, 4)


def solution(mesh):
    in_specs = (
        P("ens", None, "lat", "lon", None),
        P("ens", "lat", "lon"),
        P(), P(), P(), P(), P(), P(), P(),
    )
    out_specs = P("ens", None, "lat", "lon", None)
    return jax.shard_map(local, mesh=mesh, in_specs=in_specs, out_specs=out_specs, check_vma=False)
```

```python
import functools

import jax
import jax.numpy as jnp
from jax import lax
from jax.experimental import pallas as pl
from jax.experimental.pallas import tpu as pltpu
from jax.sharding import PartitionSpec as P

WIN_LAT = 6
WIN_LON = 12
CELL_LAT = WIN_LAT // 2
CELL_LON = WIN_LON // 2
LOG2E = 1.4426950408889634
GELU_A = 0.7978845608028654
GELU_B = GELU_A * 0.044715
F32 = jnp.float32
BF16 = jnp.bfloat16
GROUP = 256
COST = 0.6


def dot(a, b):
    return jnp.dot(a, b, preferred_element_type=F32)


def dot_t(a, b):
    return lax.dot_general(a, b, (((1,), (1,)), ((), ())), preferred_element_type=F32)


def norm_rows(values, gain_row, bias_row):
    average = jnp.mean(values, -1, keepdims=True)
    centred = values - average
    spread = jnp.mean(centred * centred, -1, keepdims=True)
    return centred * lax.rsqrt(spread + 1e-05) * gain_row + bias_row


def lane_head(rows, lanes, head_dim):
    return lax.broadcasted_iota(jnp.int32, (rows, lanes), 1) // head_dim


def scale_lanes(scale_ref, layer, width, heads):
    head_of = lane_head(1, width, width // heads)
    row = jnp.zeros((1, width), F32)
    for h in range(heads):
        row = jnp.where(head_of == h, scale_ref[layer : layer + 1, h : h + 1] * LOG2E, row)
    return row


def unit_rows(triple, scale_row, heads):
    width = triple.shape[1] // 3
    head_dim = width // heads
    ones_block = (
        lax.broadcasted_iota(jnp.int32, (GROUP, GROUP), 0) // head_dim
        == lane_head(GROUP, GROUP, head_dim)
    ).astype(BF16)
    units = []
    for at in range(0, 2 * width, GROUP):
        rows = triple[:, at : at + GROUP]
        factor = lax.rsqrt(dot(rows * rows, ones_block) + 1e-06)
        if at < width:
            factor = factor * scale_row[:, at : at + GROUP]
        units.append((rows * factor).astype(BF16))
    return units[: width // GROUP], units[width // GROUP :]


def attend(triples, scale_row, sames, heads):
    tokens, width = triples[0].shape[0], triples[0].shape[1] // 3
    head_dim = width // heads
    in_group = GROUP // head_dim
    pair_lanes = 2 * head_dim
    keys = in_group * tokens
    head_of = lane_head(1, GROUP, head_dim)
    pair_of = lane_head(1, pair_lanes, head_dim)
    one = jnp.ones((tokens, pair_lanes), BF16)
    units = [unit_rows(triple, scale_row, heads) for triple in triples]
    results = []
    for triple, (queries, key_rows), same in zip(triples, units, sames):
        pieces = []
        for g, (qn, kn) in enumerate(zip(queries, key_rows)):
            k_block = jnp.concatenate(
                [kn * (head_of == h).astype(BF16) for h in range(in_group)], axis=0
            )
            weights = jnp.exp2(dot_t(qn, k_block)).astype(BF16)
            if same is not None:
                weights = weights * same
            for p in range(in_group // 2):
                at = 2 * width + g * GROUP + p * pair_lanes
                vp = triple[:, at : at + pair_lanes]
                first = p * 2 * tokens
                start = first // 128 * 128
                stop = min(keys, -(-(first + 2 * tokens) // 128) * 128)
                rows = []
                if first > start:
                    rows.append(jnp.zeros((first - start, 2 * pair_lanes), BF16))
                for h in range(2):
                    mine = (pair_of == h).astype(BF16)
                    rows.append(jnp.concatenate([vp * mine, one * mine], axis=1))
                if stop > first + 2 * tokens:
                    rows.append(jnp.zeros((stop - first - 2 * tokens, 2 * pair_lanes), BF16))
                both = dot(weights[:, start:stop], jnp.concatenate(rows, axis=0))
                pieces.append((both[:, :pair_lanes] / both[:, pair_lanes:]).astype(BF16))
        results.append(jnp.concatenate(pieces, axis=1))
    return results


def gelu(u):
    u = u.astype(BF16)
    half = BF16(0.5) * u
    return half + half * jnp.tanh(u * (BF16(GELU_A) + BF16(GELU_B) * (u * u)))


def feed_forward(after, up_ref, down_ref, chunk):
    after_b = after.astype(BF16)
    hidden_width = up_ref.shape[1]
    total = None
    for at in range(0, hidden_width, chunk):
        h = gelu(dot(after_b, up_ref[:, at : at + chunk]))
        part = dot(h, down_ref[at : at + chunk, :])
        total = part if total is None else total + part
    return total


def feed_rows(x, attended, out_ref, up_ref, down_ref, gain_ref, bias_ref, layer):
    after = x + norm_rows(dot(attended, out_ref[...]), gain_ref[layer, 0:1], bias_ref[layer, 0:1])
    return after, feed_forward(after, up_ref, down_ref, 1024)


def first_kernel(heads, sample, has_next, more, waits, *refs):
    load = sample == 0
    refs = list(refs)

    def take(n):
        taken = refs[:n]
        del refs[:n]
        return taken

    grid_hbm, = take(1)
    given = take(7)
    if not load:
        x_ref, = take(1)
    more_hbm = take(4 if more else 0)
    take(waits)
    first_ref, east_ref, west_ref, east0_ref, west0_ref = take(5)
    next_ref = take(1)[0] if has_next else None
    held = take(7) if load else given
    more_held = take(4 if more else 0)
    if load:
        x_ref, = take(1)
    x_s, tri_s, att_s = take(3)
    next_sem = take(1)[0] if has_next else None
    rows, cols, levels, width = x_ref.shape
    x_copies, early, middle, late = [], [], [], []
    more_sems = take(1)[0] if more else None
    if load:
        x_sems, sems = take(2)
        parts = x_sems.shape[0]
        x_copies = [
            pltpu.make_async_copy(
                grid_hbm.at[0, pl.ds(n * rows // parts, rows // parts)],
                x_ref.at[pl.ds(n * rows // parts, rows // parts)],
                x_sems.at[n],
            )
            for n in range(parts)
        ]
        small = [
            pltpu.make_async_copy(given[n], held[n], sems.at[n]) for n in range(3)
        ]
        weights = [
            pltpu.make_async_copy(given[3 + n].at[0], held[3 + n], sems.at[3 + n]) for n in range(4)
        ]
        early = small[:1] + weights[:1]
        middle = small[1:] + weights[1:]
    if len(more_hbm) > 0:
        late = [
            pltpu.make_async_copy(src.at[1], dst, more_sems.at[n])
            for n, (src, dst) in enumerate(zip(more_hbm, more_held))
        ]
    if has_next:
        late = late + [pltpu.make_async_copy(grid_hbm.at[sample + 1], next_ref, next_sem.at[0])]
    for c in x_copies + early + middle:
        c.start()
    scale_ref, gain_ref, bias_ref, qkv_ref, out_ref, up_ref, down_ref = held
    bands = rows // CELL_LAT
    windows = bands // 2
    line = CELL_LON * levels
    cell = CELL_LAT * line
    for n in range(2):
        for c in x_copies[n : n + 1]:
            c.wait()
        for half in range(2):
            for r in range(n * rows // 2, (n + 1) * rows // 2):
                x_s[half, r * line : (r + 1) * line, :] = x_ref[
                    r, half * CELL_LON : (half + 1) * CELL_LON
                ].reshape(line, width)
    x = x_s[...].reshape(2 * bands * cell, width)
    for c in early:
        c.wait()
    for c in late:
        c.start()
    tri_s[...] = dot(x.astype(BF16), qkv_ref[...]).astype(BF16).reshape(tri_s.shape)
    scale_row = scale_lanes(scale_ref, 0, width, heads)
    parts = [slice(2 * cell * i, 2 * cell * (i + 1)) for i in range(windows)]
    results = attend(
        [tri_s[:, part].reshape(4 * cell, 3 * width) for part in parts],
        scale_row, [None] * windows, heads,
    )
    for part, result in zip(parts, results):
        att_s[:, part] = result.reshape(2, 2 * cell, width)
    attended = att_s[...].reshape(2 * bands * cell, width)
    for c in middle:
        c.wait()
    after, mlp = feed_rows(x, attended, out_ref, up_ref, down_ref, gain_ref, bias_ref, 0)
    first = after + norm_rows(mlp, gain_ref[0, 1:2], bias_ref[0, 1:2])
    for half in range(2):
        kept, kept0 = (west_ref, west0_ref) if half == 0 else (east_ref, east0_ref)
        for r in range(bands):
            part = first[(half * bands + r) * cell : (half * bands + r + 1) * cell]
            first_ref[half, r] = part
            if r == 0:
                kept0[...] = part.astype(BF16)
            else:
                kept[r - 1] = part.astype(BF16)
    for c in late:
        c.wait()


def shifted_kernel(
    heads,
    east_ref, west_ref, east0_ref, west0_ref, ids_ref, scale_ref, qkv_ref,
    to_east_ref, to_west_ref, to_east0_ref, to_west0_ref,
):
    cell, width = east0_ref.shape
    windows = ids_ref.shape[0] // WIN_LAT
    tokens = 4 * cell

    def cells(i, e, w, e0, w0):
        last = i == windows - 1
        return [
            e.at[2 * i],
            e0 if last else e.at[2 * i + 1],
            w.at[2 * i],
            w0 if last else w.at[2 * i + 1],
        ]

    x = jnp.concatenate(
        [
            ref[...].astype(F32)
            for i in range(windows)
            for ref in cells(i, east_ref, west_ref, east0_ref, west0_ref)
        ],
        axis=0,
    ).astype(BF16)
    triple = dot(x, qkv_ref[...]).astype(BF16)
    scale_row = scale_lanes(scale_ref, 1, width, heads)
    sames = []
    for i in range(windows):
        codes = window_codes(ids_ref, i, cell)
        sames.append(dot_t(codes, jnp.concatenate([codes] * (GROUP * heads // width), axis=0)).astype(BF16))
    results = attend(
        [triple[i * tokens : (i + 1) * tokens] for i in range(windows)], scale_row, sames, heads
    )
    for i, result in enumerate(results):
        att = result.astype(F32)
        for n, ref in enumerate(cells(i, to_east_ref, to_west_ref, to_east0_ref, to_west0_ref)):
            ref[...] = att[n * cell : (n + 1) * cell, :].astype(BF16)


def last_kernel(
    before,
    first_ref, east_ref, west_ref, east0_ref, west0_ref, gain_ref, bias_ref, out_ref, up_ref, down_ref,
    *rest,
):
    priors, rest = rest[:before], rest[before:]
    final = len(rest) > 1
    y_ref = rest[1] if final else rest[0]
    _, bands, cell, width = first_ref.shape
    line = cell // CELL_LAT
    copies = []
    if final:
        mixed_ref, _, sems = rest
        copies = [
            pltpu.make_async_copy(prior, mixed_ref.at[n], sems.at[n])
            for n, prior in enumerate(priors)
        ]
        for c in copies:
            c.start()
    pieces = []
    for half in range(2):
        kept, kept0 = (west_ref, west0_ref) if half == 0 else (east_ref, east0_ref)
        pieces.append(kept0[...].astype(F32))
        pieces.extend(kept[r].astype(F32) for r in range(bands - 1))
    attended = jnp.concatenate(pieces, axis=0).astype(BF16)
    x = first_ref[...].reshape(2 * bands * cell, width)
    after, mlp = feed_rows(x, attended, out_ref, up_ref, down_ref, gain_ref, bias_ref, 1)
    for band in range(bands):
        for half in range(2):
            at = (half * bands + band) * cell
            y = after[at : at + cell] + norm_rows(
                mlp[at : at + cell], gain_ref[1, 1:2], bias_ref[1, 1:2]
            )
            for r in range(CELL_LAT):
                y_ref[band * CELL_LAT + r, half * CELL_LON : (half + 1) * CELL_LON] = y[
                    r * line : (r + 1) * line
                ].reshape(CELL_LON, line // CELL_LON, width)
        if final:
            part = pl.ds(band * CELL_LAT, CELL_LAT)
            copies.append(
                pltpu.make_async_copy(
                    y_ref.at[part], mixed_ref.at[before, part], sems.at[before + band]
                )
            )
            copies[-1].start()
    for c in copies:
        c.wait()


ANY = pl.BlockSpec(memory_space=pl.ANY)
HBM = pl.BlockSpec(memory_space=pltpu.HBM)
SMEM = pl.BlockSpec(memory_space=pltpu.SMEM)
VMEM = pl.BlockSpec(memory_space=pltpu.VMEM)


def params(limit):
    return pltpu.CompilerParams(vmem_limit_bytes=limit << 20)


def in_hbm(array):
    return pltpu.with_memory_space_constraint(array, pltpu.HBM)


def first_layer(grid, sample, held, x, heads, more=(), after=()):
    samples, rows, cols, levels, width = grid.shape
    load = sample == 0
    has_next = sample + 1 < samples
    bands = rows // CELL_LAT
    cell = levels * CELL_LAT * CELL_LON
    kept = jax.ShapeDtypeStruct((bands - 1, cell, width), BF16)
    kept0 = jax.ShapeDtypeStruct((cell, width), BF16)
    outs = [jax.ShapeDtypeStruct((2, bands, cell, width), F32), kept, kept, kept0, kept0]
    if has_next:
        outs.append(pltpu.VMEM(grid.shape[1:], F32))
    scratch = [
        pltpu.VMEM((2, bands * cell, width), F32),
        pltpu.VMEM((2, bands * cell, 3 * width), BF16),
        pltpu.VMEM((2, bands * cell, width), BF16),
    ]
    if has_next:
        scratch.append(pltpu.SemaphoreType.DMA((1,)))
    if load:
        held = [in_hbm(h) for h in held]
        outs += [pltpu.VMEM(h.shape, h.dtype) for h in held[:3]]
        outs += [pltpu.VMEM(h.shape[1:], h.dtype) for h in held[3:]]
        scratch = [pltpu.VMEM(grid.shape[1:], F32)] + scratch
    if len(more) > 0:
        more = [in_hbm(m) for m in more]
        outs += [pltpu.VMEM(m.shape[1:], m.dtype) for m in more]
        scratch.append(pltpu.SemaphoreType.DMA((4,)))
    if load:
        scratch += [pltpu.SemaphoreType.DMA((2,)), pltpu.SemaphoreType.DMA((7,))]
    ins = [] if load else [x]
    return pl.pallas_call(
        functools.partial(first_kernel, heads, sample, has_next, len(more) > 0, len(after)),
        in_specs=[HBM] + [HBM if load else VMEM] * 7 + [VMEM] * len(ins) + [HBM] * len(more) + [ANY] * len(after),
        out_specs=[VMEM] * len(outs),
        out_shape=outs,
        scratch_shapes=scratch,
        compiler_params=params(16),
        cost_estimate=pl.CostEstimate(flops=int(8e9*COST), bytes_accessed=int(10e6*COST), transcendentals=0),
        name="first_layer",
    )(in_hbm(grid), *held, *ins, *more, *after)


def shifted_attention(east, west, east0, west0, ids, scale, qkv, heads):
    args = (east, west, east0, west0)
    return pl.pallas_call(
        functools.partial(shifted_kernel, heads),
        in_specs=[VMEM] * 4 + [SMEM, VMEM, VMEM],
        out_specs=[VMEM] * 4,
        out_shape=[jax.ShapeDtypeStruct(a.shape, BF16) for a in args],
        compiler_params=params(16),
        cost_estimate=pl.CostEstimate(flops=int(4e9*COST), bytes_accessed=int(5e6*COST), transcendentals=0),
        name="shifted_attention",
    )(*args, ids, scale, qkv)


def last_half(first, east, west, east0, west0, gain, bias, out, up, down, priors, shape):
    sample = len(priors)
    final = sample + 1 == shape[0]
    used = priors if final else []
    y = pltpu.VMEM(shape[1:], F32)
    return pl.pallas_call(
        functools.partial(last_kernel, len(used)),
        in_specs=[VMEM] * (10 + len(used)),
        out_specs=HBM if final else VMEM,
        out_shape=jax.ShapeDtypeStruct(shape, F32) if final else y,
        scratch_shapes=[y, pltpu.SemaphoreType.DMA((sample + first.shape[1],))] if final else [],
        compiler_params=params(14),
        cost_estimate=pl.CostEstimate(flops=int(4e9*COST), bytes_accessed=int(5e6*COST), transcendentals=0),
        name="last_half",
    )(first, east, west, east0, west0, gain, bias, out, up, down, *used)


def shifted(x, lat_by, lon_by):
    lat, lon = lax.axis_size("lat"), lax.axis_size("lon")
    pairs = [
        (o * lat + a, (o + lon_by) % lon * lat + (a + lat_by) % lat)
        for o in range(lon)
        for a in range(lat)
    ]
    return lax.ppermute(x, ("lon", "lat"), pairs)


def window_codes(ids_ref, window, cell):
    rows, levels, _ = ids_ref.shape
    lat_total = lax.axis_size("lat") * rows
    start = lax.axis_index("lat") * rows + window * WIN_LAT
    token = lax.broadcasted_iota(jnp.int32, (cell, 128), 0)
    column = lax.rem(token // levels, CELL_LON)
    lane = lax.broadcasted_iota(jnp.int32, (cell, 128), 1)
    codes = []
    for half in range(2):
        ids = jnp.zeros((cell, 128), jnp.int32)
        for c in range(CELL_LON):
            ids = jnp.where(column == c, ids_ref[window * WIN_LAT, 0, half * CELL_LON + c], ids)
        for r in range(2):
            at = start + r * CELL_LAT
            band = jnp.where(at >= lat_total - WIN_LAT, 1, 0) + jnp.where(
                at >= lat_total - CELL_LAT, 1, 0
            )
            codes.append(jnp.where(ids * 3 + band == lane, 1.0, 0.0))
    return jnp.concatenate(codes, axis=0).astype(BF16)


def local(stream, region_ids, qkv, out, up, down, gain, bias, scale):
    samples = stream.shape[0]
    heads = scale.shape[1]
    ids = region_ids.transpose(1, 0, 2)
    grid = stream.transpose(0, 2, 3, 1, 4)
    weights = [qkv, out, up, down]
    held = [scale, gain, bias] + weights
    firsts, halos, backs, x = [], [], [], None

    def attention(s):
        east, west, east0, west0 = shifted_attention(*halos[s], ids, held[0], later[0], heads)
        backs.append((east, shifted(west, 0, 1), shifted(east0, 1, 0), shifted(west0, 1, 1)))
        return [east0]

    for s in range(samples):
        after = attention(s - 2) if s >= 2 else ()
        more = weights if s == min(1, samples - 1) else ()
        made = first_layer(grid, s, held, x, heads, more, after)
        first, east, west, east0, west0 = made[:5]
        made = made[5:]
        if s + 1 < samples:
            x, made = made[0], made[1:]
        if s == 0:
            held, made = made[:7], made[7:]
        if len(more) > 0:
            later = made
        firsts.append(first)
        halos.append((east, shifted(west, 0, -1), shifted(east0, -1, 0), shifted(west0, -1, -1)))
    for s in range(max(samples - 2, 0), samples):
        attention(s)
    mixed = []
    for s in range(samples):
        mixed.append(last_half(firsts[s], *backs[s], *held[1:3], *later[1:], mixed, grid.shape))
    return mixed[-1].transpose(0, 3, 1, 2, 4)


def solution(mesh):
    in_specs = (
        P("ens", None, "lat", "lon", None),
        P("ens", "lat", "lon"),
        P(), P(), P(), P(), P(), P(), P(),
    )
    out_specs = P("ens", None, "lat", "lon", None)
    return jax.shard_map(local, mesh=mesh, in_specs=in_specs, out_specs=out_specs, check_vma=False)
```

```python
import functools

import jax
import jax.numpy as jnp
from jax import lax
from jax.experimental import pallas as pl
from jax.experimental.pallas import tpu as pltpu
from jax.sharding import PartitionSpec as P

WIN_LAT = 6
WIN_LON = 12
CELL_LAT = WIN_LAT // 2
CELL_LON = WIN_LON // 2
LOG2E = 1.4426950408889634
GELU_A = 0.7978845608028654
GELU_B = GELU_A * 0.044715
F32 = jnp.float32
BF16 = jnp.bfloat16
GROUP = 256
COST = 0.6


def dot(a, b):
    return jnp.dot(a, b, preferred_element_type=F32)


def dot_t(a, b):
    return lax.dot_general(a, b, (((1,), (1,)), ((), ())), preferred_element_type=F32)


def norm_rows(values, gain_row, bias_row):
    average = jnp.mean(values, -1, keepdims=True)
    centred = values - average
    spread = jnp.mean(centred * centred, -1, keepdims=True)
    return centred * lax.rsqrt(spread + 1e-05) * gain_row + bias_row


def lane_head(rows, lanes, head_dim):
    return lax.broadcasted_iota(jnp.int32, (rows, lanes), 1) // head_dim


def scale_lanes(scale_ref, layer, width, heads):
    head_of = lane_head(1, width, width // heads)
    row = jnp.zeros((1, width), F32)
    for h in range(heads):
        row = jnp.where(head_of == h, scale_ref[layer : layer + 1, h : h + 1] * LOG2E, row)
    return row


def unit_rows(triple, scale_row, heads):
    width = triple.shape[1] // 3
    head_dim = width // heads
    ones_block = (
        lax.broadcasted_iota(jnp.int32, (GROUP, GROUP), 0) // head_dim
        == lane_head(GROUP, GROUP, head_dim)
    ).astype(BF16)
    units = []
    for at in range(0, 2 * width, GROUP):
        rows = triple[:, at : at + GROUP]
        factor = lax.rsqrt(dot(rows * rows, ones_block) + 1e-06)
        if at < width:
            factor = factor * scale_row[:, at : at + GROUP]
        units.append((rows * factor).astype(BF16))
    return units[: width // GROUP], units[width // GROUP :]


def attend(triples, scale_row, sames, heads):
    tokens, width = triples[0].shape[0], triples[0].shape[1] // 3
    head_dim = width // heads
    in_group = GROUP // head_dim
    pair_lanes = 2 * head_dim
    keys = in_group * tokens
    head_of = lane_head(1, GROUP, head_dim)
    pair_of = lane_head(1, pair_lanes, head_dim)
    one = jnp.ones((tokens, pair_lanes), BF16)
    units = [unit_rows(triple, scale_row, heads) for triple in triples]
    results = []
    for triple, (queries, key_rows), same in zip(triples, units, sames):
        pieces = []
        for g, (qn, kn) in enumerate(zip(queries, key_rows)):
            k_block = jnp.concatenate(
                [kn * (head_of == h).astype(BF16) for h in range(in_group)], axis=0
            )
            weights = jnp.exp2(dot_t(qn, k_block)).astype(BF16)
            if same is not None:
                weights = weights * same
            for p in range(in_group // 2):
                at = 2 * width + g * GROUP + p * pair_lanes
                vp = triple[:, at : at + pair_lanes]
                first = p * 2 * tokens
                start = first // 128 * 128
                stop = min(keys, -(-(first + 2 * tokens) // 128) * 128)
                rows = []
                if first > start:
                    rows.append(jnp.zeros((first - start, 2 * pair_lanes), BF16))
                for h in range(2):
                    mine = (pair_of == h).astype(BF16)
                    rows.append(jnp.concatenate([vp * mine, one * mine], axis=1))
                if stop > first + 2 * tokens:
                    rows.append(jnp.zeros((stop - first - 2 * tokens, 2 * pair_lanes), BF16))
                both = dot(weights[:, start:stop], jnp.concatenate(rows, axis=0))
                pieces.append((both[:, :pair_lanes] / both[:, pair_lanes:]).astype(BF16))
        results.append(jnp.concatenate(pieces, axis=1))
    return results


def gelu(u):
    u = u.astype(BF16)
    half = BF16(0.5) * u
    return half + half * jnp.tanh(u * (BF16(GELU_A) + BF16(GELU_B) * (u * u)))


def feed_forward(after, up_ref, down_ref, chunk):
    after_b = after.astype(BF16)
    hidden_width = up_ref.shape[1]
    total = None
    for at in range(0, hidden_width, chunk):
        h = gelu(dot(after_b, up_ref[:, at : at + chunk]))
        part = dot(h, down_ref[at : at + chunk, :])
        total = part if total is None else total + part
    return total


def feed_rows(x, attended, out_ref, up_ref, down_ref, gain_ref, bias_ref, layer):
    after = x + norm_rows(dot(attended, out_ref[...]), gain_ref[layer, 0:1], bias_ref[layer, 0:1])
    return after, feed_forward(after, up_ref, down_ref, 1024)


def first_kernel(heads, sample, has_next, more, carries, waits, *refs):
    load = sample == 0
    refs = list(refs)

    def take(n):
        taken = refs[:n]
        del refs[:n]
        return taken

    grid_hbm, = take(1)
    given = take(7)
    if not load:
        x_ref, = take(1)
    more_hbm = take(4 if more else 0)
    carried = take(carries)
    take(waits)
    first_ref, east_ref, west_ref, east0_ref, west0_ref = take(5)
    next_ref = take(1)[0] if has_next else None
    held = take(7) if load else given
    more_held = take(4 if more else 0)
    if load:
        x_ref, = take(1)
    x_s, tri_s, att_s = take(3)
    next_sem = take(1)[0] if has_next else None
    rows, cols, levels, width = x_ref.shape
    x_copies, early, middle, late = [], [], [], []
    more_sems = take(1)[0] if more else None
    if load:
        x_sems, sems = take(2)
        parts = x_sems.shape[0]
        x_copies = [
            pltpu.make_async_copy(
                grid_hbm.at[0, pl.ds(n * rows // parts, rows // parts)],
                x_ref.at[pl.ds(n * rows // parts, rows // parts)],
                x_sems.at[n],
            )
            for n in range(parts)
        ]
        small = [
            pltpu.make_async_copy(given[n], held[n], sems.at[n]) for n in range(3)
        ]
        weights = [
            pltpu.make_async_copy(given[3 + n].at[0], held[3 + n], sems.at[3 + n]) for n in range(4)
        ]
        early = small[:1] + weights[:1]
        middle = small[1:] + weights[1:]
    if len(more_hbm) > 0:
        late = [
            pltpu.make_async_copy(src.at[1], dst, more_sems.at[n])
            for n, (src, dst) in enumerate(zip(more_hbm, more_held))
        ]
    if has_next:
        late = late + [pltpu.make_async_copy(grid_hbm.at[sample + 1], next_ref, next_sem.at[0])]
    for c in x_copies + early:
        c.start()
    scale_ref, gain_ref, bias_ref, qkv_ref, out_ref, up_ref, down_ref = held
    bands = rows // CELL_LAT
    windows = bands // 2
    line = CELL_LON * levels
    cell = CELL_LAT * line
    for n in range(2):
        for c in x_copies[n : n + 1]:
            c.wait()
        for half in range(2):
            for r in range(n * rows // 2, (n + 1) * rows // 2):
                x_s[half, r * line : (r + 1) * line, :] = x_ref[
                    r, half * CELL_LON : (half + 1) * CELL_LON
                ].reshape(line, width)
    x = x_s[...].reshape(2 * bands * cell, width)
    for c in early:
        c.wait()
    for c in middle + late:
        c.start()
    tri_s[...] = dot(x.astype(BF16), qkv_ref[...]).astype(BF16).reshape(tri_s.shape)
    scale_row = scale_lanes(scale_ref, 0, width, heads)
    parts = [slice(2 * cell * i, 2 * cell * (i + 1)) for i in range(windows)]
    results = attend(
        [tri_s[:, part].reshape(4 * cell, 3 * width) for part in parts],
        scale_row, [None] * windows, heads,
    )
    for part, result in zip(parts, results):
        att_s[:, part] = result.reshape(2, 2 * cell, width)
    attended = att_s[...].reshape(2 * bands * cell, width)
    for c in middle:
        c.wait()
    after, mlp = feed_rows(x, attended, out_ref, up_ref, down_ref, gain_ref, bias_ref, 0)
    first = after + norm_rows(mlp, gain_ref[0, 1:2], bias_ref[0, 1:2])
    for half in range(2):
        kept, kept0 = (west_ref, west0_ref) if half == 0 else (east_ref, east0_ref)
        for r in range(bands):
            part = first[(half * bands + r) * cell : (half * bands + r + 1) * cell]
            first_ref[half, r] = part
            if r == 0:
                kept0[kept0.shape[0] - 1] = part.astype(BF16)
            else:
                kept[r - 1] = part.astype(BF16)
    for kept0, old in zip((east0_ref, west0_ref), carried):
        kept0[0] = old[0]
    for c in late:
        c.wait()


def shifted_kernel(
    heads, make, at0, carries, waits,
    east_ref, west_ref, east0_ref, west0_ref, ids_ref, scale_ref, qkv_ref,
    *rest,
):
    carried, rest = rest[:carries], rest[carries + waits :]
    to_east_ref, to_west_ref, to_east0_ref, to_west0_ref = rest[:4]
    for to, old in zip((to_east0_ref, to_west0_ref), carried):
        to[0] = old[0]
    east0_ref, west0_ref = east0_ref.at[at0], west0_ref.at[at0]
    to_east0_ref = to_east0_ref.at[to_east0_ref.shape[0] - 1]
    to_west0_ref = to_west0_ref.at[to_west0_ref.shape[0] - 1]
    cell, width = east0_ref.shape
    tokens = 4 * cell
    if make:
        same_ref = rest[-1]
        windows = ids_ref.shape[0] // WIN_LAT
        for i in range(windows):
            codes = window_codes(ids_ref, i, cell)
            same_ref[i] = dot_t(
                codes, jnp.concatenate([codes] * (GROUP * heads // width), axis=0)
            ).astype(BF16)
    else:
        same_ref = ids_ref
        windows = same_ref.shape[0]

    def cells(i, e, w, e0, w0):
        last = i == windows - 1
        return [
            e.at[2 * i],
            e0 if last else e.at[2 * i + 1],
            w.at[2 * i],
            w0 if last else w.at[2 * i + 1],
        ]

    x = jnp.concatenate(
        [
            ref[...].astype(F32)
            for i in range(windows)
            for ref in cells(i, east_ref, west_ref, east0_ref, west0_ref)
        ],
        axis=0,
    ).astype(BF16)
    triple = dot(x, qkv_ref[...]).astype(BF16)
    scale_row = scale_lanes(scale_ref, 1, width, heads)
    sames = [same_ref[i] for i in range(windows)]
    results = attend(
        [triple[i * tokens : (i + 1) * tokens] for i in range(windows)], scale_row, sames, heads
    )
    for i, result in enumerate(results):
        att = result.astype(F32)
        for n, ref in enumerate(cells(i, to_east_ref, to_west_ref, to_east0_ref, to_west0_ref)):
            ref[...] = att[n * cell : (n + 1) * cell, :].astype(BF16)


def last_kernel(halves, at0s, before, waits, *refs):
    refs = list(refs)
    jobs = [refs[3 * n : 3 * n + 3] for n in range(len(halves))]
    refs = refs[3 * len(halves) :]
    gain_ref, bias_ref, out_ref, up_ref, down_ref = refs[:5]
    priors, refs = refs[5 : 5 + len(before)], refs[5 + len(before) + waits :]
    final = len(before) > 0
    _, bands, cell, width = jobs[0][0].shape
    line = cell // CELL_LAT
    copies = []
    if final:
        mixed_ref, *y_refs, sems = refs
        columns = [pl.ds(half * CELL_LON, CELL_LON) for half in range(2)]
        for n, (prior, (sample, half)) in enumerate(zip(priors, before)):
            copies.append(
                pltpu.make_async_copy(prior, mixed_ref.at[sample, :, columns[half]], sems.at[n])
            )
            copies[-1].start()
    else:
        y_refs = refs
    pieces, rows = [], []
    for (sample, half), at0, (first_ref, kept, kept0) in zip(halves, at0s, jobs):
        pieces.append(kept0[at0].astype(F32))
        pieces.extend(kept[r].astype(F32) for r in range(bands - 1))
        rows.append(first_ref[half].reshape(bands * cell, width))
    attended = jnp.concatenate(pieces, axis=0).astype(BF16)
    x = jnp.concatenate(rows, axis=0)
    after, mlp = feed_rows(x, attended, out_ref, up_ref, down_ref, gain_ref, bias_ref, 1)
    for n, ((sample, half), y_ref) in enumerate(zip(halves, y_refs)):
        for band in range(bands):
            at = (n * bands + band) * cell
            y = after[at : at + cell] + norm_rows(
                mlp[at : at + cell], gain_ref[1, 1:2], bias_ref[1, 1:2]
            )
            part = pl.ds(band * CELL_LAT, CELL_LAT)
            y_ref[part] = y.reshape(CELL_LAT, CELL_LON, line // CELL_LON, width)
            if final:
                copies.append(
                    pltpu.make_async_copy(
                        y_ref.at[part],
                        mixed_ref.at[sample, part, columns[half]],
                        sems.at[len(copies)],
                    )
                )
                copies[-1].start()
    for c in copies:
        c.wait()


ANY = pl.BlockSpec(memory_space=pl.ANY)
HBM = pl.BlockSpec(memory_space=pltpu.HBM)
SMEM = pl.BlockSpec(memory_space=pltpu.SMEM)
VMEM = pl.BlockSpec(memory_space=pltpu.VMEM)


def params(limit):
    return pltpu.CompilerParams(vmem_limit_bytes=limit << 20)


def in_hbm(array):
    return pltpu.with_memory_space_constraint(array, pltpu.HBM)


def first_layer(grid, sample, held, x, heads, more=(), carried=(), after=()):
    samples, rows, cols, levels, width = grid.shape
    load = sample == 0
    has_next = sample + 1 < samples
    bands = rows // CELL_LAT
    cell = levels * CELL_LAT * CELL_LON
    kept = jax.ShapeDtypeStruct((bands - 1, cell, width), BF16)
    kept0 = jax.ShapeDtypeStruct((1 + len(carried) // 2, cell, width), BF16)
    outs = [jax.ShapeDtypeStruct((2, bands, cell, width), F32), kept, kept, kept0, kept0]
    if has_next:
        outs.append(pltpu.VMEM(grid.shape[1:], F32))
    scratch = [
        pltpu.VMEM((2, bands * cell, width), F32),
        pltpu.VMEM((2, bands * cell, 3 * width), BF16),
        pltpu.VMEM((2, bands * cell, width), BF16),
    ]
    if has_next:
        scratch.append(pltpu.SemaphoreType.DMA((1,)))
    if load:
        held = [in_hbm(h) for h in held]
        outs += [pltpu.VMEM(h.shape, h.dtype) for h in held[:3]]
        outs += [pltpu.VMEM(h.shape[1:], h.dtype) for h in held[3:]]
        scratch = [pltpu.VMEM(grid.shape[1:], F32)] + scratch
    if len(more) > 0:
        more = [in_hbm(m) for m in more]
        outs += [pltpu.VMEM(m.shape[1:], m.dtype) for m in more]
        scratch.append(pltpu.SemaphoreType.DMA((4,)))
    if load:
        scratch += [pltpu.SemaphoreType.DMA((2,)), pltpu.SemaphoreType.DMA((7,))]
    ins = [] if load else [x]
    return pl.pallas_call(
        functools.partial(first_kernel, heads, sample, has_next, len(more) > 0, len(carried), len(after)),
        in_specs=[HBM] + [HBM if load else VMEM] * 7 + [VMEM] * len(ins) + [HBM] * len(more) + [VMEM] * len(carried) + [ANY] * len(after),
        out_specs=[VMEM] * len(outs),
        out_shape=outs,
        scratch_shapes=scratch,
        compiler_params=params(16),
        cost_estimate=pl.CostEstimate(flops=int(8e9*COST), bytes_accessed=int(10e6*COST), transcendentals=0),
        name="first_layer",
    )(in_hbm(grid), *held, *ins, *more, *carried, *after)


def shifted_attention(east, west, east0, west0, at0, ids, scale, qkv, heads, make, carried=(), after=()):
    args = (east, west, east0, west0)
    cell, width = east.shape[1:]
    kept = jax.ShapeDtypeStruct(east.shape, BF16)
    kept0 = jax.ShapeDtypeStruct((1 + len(carried) // 2, cell, width), BF16)
    outs = [kept, kept, kept0, kept0]
    if make:
        tokens = 4 * cell
        keys = tokens * (GROUP * heads // width)
        outs.append(pltpu.VMEM((ids.shape[0] // WIN_LAT, tokens, keys), BF16))
    return pl.pallas_call(
        functools.partial(shifted_kernel, heads, make, at0, len(carried), len(after)),
        in_specs=[VMEM] * 4 + [SMEM if make else VMEM, VMEM, VMEM] + [VMEM] * len(carried) + [ANY] * len(after),
        out_specs=[VMEM] * len(outs),
        out_shape=outs,
        compiler_params=params(16),
        cost_estimate=pl.CostEstimate(flops=int(4e9*COST), bytes_accessed=int(5e6*COST), transcendentals=0),
        name="shifted_attention",
    )(*args, ids, scale, qkv, *carried, *after)


def last_half(halves, jobs, at0s, held, shape, priors=None, after=()):
    _, rows, cols, levels, width = shape
    priors = priors or {}
    final = len(priors) > 0
    y = pltpu.VMEM((rows, CELL_LON, levels, width), F32)
    ys = [y] * len(halves)
    bands = rows // CELL_LAT
    operands = [array for job in jobs for array in job]
    outs = [jax.ShapeDtypeStruct(shape, F32)] if final else ys
    copies = len(priors) + bands * len(halves)
    size = len(halves) / 2 * COST
    return pl.pallas_call(
        functools.partial(last_kernel, tuple(halves), tuple(at0s), tuple(priors), len(after)),
        in_specs=[VMEM] * (len(operands) + 5 + len(priors)) + [ANY] * len(after),
        out_specs=[HBM if final else VMEM] * len(outs),
        out_shape=outs,
        scratch_shapes=ys + [pltpu.SemaphoreType.DMA((copies,))] if final else [],
        compiler_params=params(18),
        cost_estimate=pl.CostEstimate(flops=int(5e9*size), bytes_accessed=int(5e6*size), transcendentals=0),
        name="last_half",
    )(*operands, *held, *priors.values(), *after)


def shifted(x, lat_by, lon_by):
    lat, lon = lax.axis_size("lat"), lax.axis_size("lon")
    pairs = [
        (o * lat + a, (o + lon_by) % lon * lat + (a + lat_by) % lat)
        for o in range(lon)
        for a in range(lat)
    ]
    return lax.ppermute(x, ("lon", "lat"), pairs)


def window_codes(ids_ref, window, cell):
    rows, levels, _ = ids_ref.shape
    lat_total = lax.axis_size("lat") * rows
    start = lax.axis_index("lat") * rows + window * WIN_LAT
    token = lax.broadcasted_iota(jnp.int32, (cell, 128), 0)
    column = lax.rem(token // levels, CELL_LON)
    lane = lax.broadcasted_iota(jnp.int32, (cell, 128), 1)
    codes = []
    for half in range(2):
        ids = jnp.zeros((cell, 128), jnp.int32)
        for c in range(CELL_LON):
            ids = jnp.where(column == c, ids_ref[window * WIN_LAT, 0, half * CELL_LON + c], ids)
        for r in range(2):
            at = start + r * CELL_LAT
            band = jnp.where(at >= lat_total - WIN_LAT, 1, 0) + jnp.where(
                at >= lat_total - CELL_LAT, 1, 0
            )
            codes.append(jnp.where(ids * 3 + band == lane, 1.0, 0.0))
    return jnp.concatenate(codes, axis=0).astype(BF16)


def local(stream, region_ids, qkv, out, up, down, gain, bias, scale):
    samples = stream.shape[0]
    heads = scale.shape[1]
    ids = region_ids.transpose(1, 0, 2)
    grid = stream.transpose(0, 2, 3, 1, 4)
    weights = [qkv, out, up, down]
    held = [scale, gain, bias] + weights
    firsts, halos, backs, same, x = [], [], [], [], None
    place = [max(s, 1) for s in range(samples)] if samples > 1 else [0]
    at0s = [1 if s == 1 else 0 for s in range(samples)]
    sent0, back0 = {}, {}
    for s in range(samples):
        after = [halos[s - 2][1]] if s >= 2 else ()
        more = weights if s == min(1, samples - 1) else ()
        carried = made0 if s == 1 else ()
        made = first_layer(grid, s, held, x, heads, more, carried, after)
        first, east, west, *made0 = made[:5]
        made = made[5:]
        if s + 1 < samples:
            x, made = made[0], made[1:]
        if s == 0:
            held, made = made[:7], made[7:]
        if len(more) > 0:
            later = made
        firsts.append(first)
        if place[s] == s:
            sent0[s] = (shifted(made0[0], -1, 0), shifted(made0[1], -1, -1))
        halos.append((east, shifted(west, 0, -1)))
    for s in range(samples):
        after = [halos[1][1]] if s == 0 and samples > 1 else [b[1] for b in backs[s - 2 : s - 1]]
        keys = same[0] if len(same) > 0 else ids
        carried = made0 if s == 1 else ()
        east, west, *made0 = shifted_attention(
            *halos[s], *sent0[place[s]], at0s[s], keys, held[0], later[0], heads,
            len(same) == 0, carried, after,
        )
        made0, more = made0[:2], made0[2:]
        same.extend(more)
        if place[s] == s:
            back0[s] = (shifted(made0[0], 1, 0), shifted(made0[1], 1, 1))
        backs.append((east, shifted(west, 0, 1)))
    feed = [*held[1:3], *later[1:]]
    groups = [[(s, 0), (s, 1)] for s in range(samples - 1)]
    if len(groups) == 0:
        groups.append([])
    groups[-1].append((samples - 1, 1))
    groups.append([(samples - 1, 0)])
    made, ys = {}, ()
    for n, halves in enumerate(groups):
        jobs = []
        for s, half in halves:
            east0, west0 = back0[place[s]]
            jobs.append((firsts[s], backs[s][1], west0) if half == 0 else (firsts[s], backs[s][0], east0))
        final = n == len(groups) - 1
        ys = last_half(halves, jobs, [at0s[s] for s, _ in halves], feed, grid.shape, made if final else None, () if final else ys[:1])
        made.update(zip(halves, ys))
    return ys[0].transpose(0, 3, 1, 2, 4)


def solution(mesh):
    in_specs = (
        P("ens", None, "lat", "lon", None),
        P("ens", "lat", "lon"),
        P(), P(), P(), P(), P(), P(), P(),
    )
    out_specs = P("ens", None, "lat", "lon", None)
    return jax.shard_map(local, mesh=mesh, in_specs=in_specs, out_specs=out_specs, check_vma=False)
```

```python
import functools

import jax
import jax.numpy as jnp
from jax import lax
from jax.experimental import pallas as pl
from jax.experimental.pallas import tpu as pltpu
from jax.sharding import PartitionSpec as P

WIN_LAT = 6
WIN_LON = 12
CELL_LAT = WIN_LAT // 2
CELL_LON = WIN_LON // 2
LOG2E = 1.4426950408889634
GELU_A = 0.7978845608028654
GELU_B = GELU_A * 0.044715
F32 = jnp.float32
BF16 = jnp.bfloat16
GROUP = 256
COST = 0.6


def dot(a, b):
    return jnp.dot(a, b, preferred_element_type=F32)


def dot_t(a, b):
    return lax.dot_general(a, b, (((1,), (1,)), ((), ())), preferred_element_type=F32)


def norm_rows(values, gain_row, bias_row):
    average = jnp.mean(values, -1, keepdims=True)
    centred = values - average
    spread = jnp.mean(centred * centred, -1, keepdims=True)
    return centred * lax.rsqrt(spread + 1e-05) * gain_row + bias_row


def lane_head(rows, lanes, head_dim):
    return lax.broadcasted_iota(jnp.int32, (rows, lanes), 1) // head_dim


def scale_lanes(scale_ref, layer, width, heads):
    head_of = lane_head(1, width, width // heads)
    row = jnp.zeros((1, width), F32)
    for h in range(heads):
        row = jnp.where(head_of == h, scale_ref[layer : layer + 1, h : h + 1] * LOG2E, row)
    return row


def unit_rows(triple, scale_row, heads):
    width = triple.shape[1] // 3
    head_dim = width // heads
    ones_block = (
        lax.broadcasted_iota(jnp.int32, (GROUP, GROUP), 0) // head_dim
        == lane_head(GROUP, GROUP, head_dim)
    ).astype(BF16)
    units = []
    for at in range(0, 2 * width, GROUP):
        rows = triple[:, at : at + GROUP]
        factor = lax.rsqrt(dot(rows * rows, ones_block) + 1e-06)
        if at < width:
            factor = factor * scale_row[:, at : at + GROUP]
        units.append((rows * factor).astype(BF16))
    return units[: width // GROUP], units[width // GROUP :]


def attend(triples, scale_row, sames, heads):
    tokens, width = triples[0].shape[0], triples[0].shape[1] // 3
    head_dim = width // heads
    in_group = GROUP // head_dim
    pair_lanes = 2 * head_dim
    keys = in_group * tokens
    head_of = lane_head(1, GROUP, head_dim)
    pair_of = lane_head(1, pair_lanes, head_dim)
    one = jnp.ones((tokens, pair_lanes), BF16)
    units = [unit_rows(triple, scale_row, heads) for triple in triples]
    results = []
    for triple, (queries, key_rows), same in zip(triples, units, sames):
        pieces = []
        for g, (qn, kn) in enumerate(zip(queries, key_rows)):
            k_block = jnp.concatenate(
                [kn * (head_of == h).astype(BF16) for h in range(in_group)], axis=0
            )
            weights = jnp.exp2(dot_t(qn, k_block)).astype(BF16)
            if same is not None:
                weights = weights * same
            for p in range(in_group // 2):
                at = 2 * width + g * GROUP + p * pair_lanes
                vp = triple[:, at : at + pair_lanes]
                first = p * 2 * tokens
                start = first // 128 * 128
                stop = min(keys, -(-(first + 2 * tokens) // 128) * 128)
                rows = []
                if first > start:
                    rows.append(jnp.zeros((first - start, 2 * pair_lanes), BF16))
                for h in range(2):
                    mine = (pair_of == h).astype(BF16)
                    rows.append(jnp.concatenate([vp * mine, one * mine], axis=1))
                if stop > first + 2 * tokens:
                    rows.append(jnp.zeros((stop - first - 2 * tokens, 2 * pair_lanes), BF16))
                both = dot(weights[:, start:stop], jnp.concatenate(rows, axis=0))
                pieces.append((both[:, :pair_lanes] / both[:, pair_lanes:]).astype(BF16))
        results.append(jnp.concatenate(pieces, axis=1))
    return results


def gelu(u):
    u = u.astype(BF16)
    half = BF16(0.5) * u
    return half + half * jnp.tanh(u * (BF16(GELU_A) + BF16(GELU_B) * (u * u)))


def feed_forward(after, up_ref, down_ref, chunk):
    after_b = after.astype(BF16)
    hidden_width = up_ref.shape[1]
    total = None
    for at in range(0, hidden_width, chunk):
        h = gelu(dot(after_b, up_ref[:, at : at + chunk]))
        part = dot(h, down_ref[at : at + chunk, :])
        total = part if total is None else total + part
    return total


def feed_rows(x, attended, out_ref, up_ref, down_ref, gain_ref, bias_ref, layer):
    after = x + norm_rows(dot(attended, out_ref[...]), gain_ref[layer, 0:1], bias_ref[layer, 0:1])
    return after, feed_forward(after, up_ref, down_ref, 1024)


def first_kernel(heads, sample, has_next, more, carries, waits, *refs):
    load = sample == 0
    refs = list(refs)

    def take(n):
        taken = refs[:n]
        del refs[:n]
        return taken

    grid_hbm, = take(1)
    given = take(7)
    if not load:
        x_ref, = take(1)
    more_hbm = take(4 if more else 0)
    carried = take(carries)
    take(waits)
    first_ref, east_ref, west_ref, east0_ref, west0_ref = take(5)
    next_ref = take(1)[0] if has_next else None
    held = take(7) if load else given
    more_held = take(4 if more else 0)
    if load:
        x_ref, = take(1)
    x_s, tri_s, att_s = take(3)
    next_sem = take(1)[0] if has_next else None
    rows, cols, levels, width = x_ref.shape
    x_copies, early, middle, late = [], [], [], []
    more_sems = take(1)[0] if more else None
    if load:
        x_sems, sems = take(2)
        parts = x_sems.shape[0]
        x_copies = [
            pltpu.make_async_copy(
                grid_hbm.at[0, pl.ds(n * rows // parts, rows // parts)],
                x_ref.at[pl.ds(n * rows // parts, rows // parts)],
                x_sems.at[n],
            )
            for n in range(parts)
        ]
        small = [
            pltpu.make_async_copy(given[n], held[n], sems.at[n]) for n in range(3)
        ]
        weights = [
            pltpu.make_async_copy(given[3 + n].at[0], held[3 + n], sems.at[3 + n]) for n in range(4)
        ]
        early = small[:1] + weights[:1]
        middle = small[1:] + weights[1:]
    if len(more_hbm) > 0:
        late = [
            pltpu.make_async_copy(src.at[1], dst, more_sems.at[n])
            for n, (src, dst) in enumerate(zip(more_hbm, more_held))
        ]
    if has_next:
        late = late + [pltpu.make_async_copy(grid_hbm.at[sample + 1], next_ref, next_sem.at[0])]
    for c in x_copies + early:
        c.start()
    scale_ref, gain_ref, bias_ref, qkv_ref, out_ref, up_ref, down_ref = held
    bands = rows // CELL_LAT
    windows = bands // 2
    line = CELL_LON * levels
    cell = CELL_LAT * line
    for n in range(2):
        for c in x_copies[n : n + 1]:
            c.wait()
        for half in range(2):
            for r in range(n * rows // 2, (n + 1) * rows // 2):
                x_s[half, r * line : (r + 1) * line, :] = x_ref[
                    r, half * CELL_LON : (half + 1) * CELL_LON
                ].reshape(line, width)
    x = x_s[...].reshape(2 * bands * cell, width)
    for c in early:
        c.wait()
    for c in middle + late:
        c.start()
    tri_s[...] = dot(x.astype(BF16), qkv_ref[...]).astype(BF16).reshape(tri_s.shape)
    scale_row = scale_lanes(scale_ref, 0, width, heads)
    parts = [slice(2 * cell * i, 2 * cell * (i + 1)) for i in range(windows)]
    results = attend(
        [tri_s[:, part].reshape(4 * cell, 3 * width) for part in parts],
        scale_row, [None] * windows, heads,
    )
    for part, result in zip(parts, results):
        att_s[:, part] = result.reshape(2, 2 * cell, width)
    attended = att_s[...].reshape(2 * bands * cell, width)
    for c in middle:
        c.wait()
    after, mlp = feed_rows(x, attended, out_ref, up_ref, down_ref, gain_ref, bias_ref, 0)
    first = after + norm_rows(mlp, gain_ref[0, 1:2], bias_ref[0, 1:2])
    for half in range(2):
        kept, kept0 = (west_ref, west0_ref) if half == 0 else (east_ref, east0_ref)
        for r in range(bands):
            part = first[(half * bands + r) * cell : (half * bands + r + 1) * cell]
            first_ref[half, r] = part
            if r == 0:
                kept0[kept0.shape[0] - 1] = part.astype(BF16)
            else:
                kept[r - 1] = part.astype(BF16)
    for kept0, old in zip((east0_ref, west0_ref), carried):
        kept0[0] = old[0]
    for c in late:
        c.wait()


def shifted_kernel(
    heads, make, at0, carries, waits,
    east_ref, west_ref, east0_ref, west0_ref, ids_ref, scale_ref, qkv_ref,
    *rest,
):
    carried, rest = rest[:carries], rest[carries + waits :]
    to_east_ref, to_west_ref, to_east0_ref, to_west0_ref = rest[:4]
    for to, old in zip((to_east0_ref, to_west0_ref), carried):
        to[0] = old[0]
    east0_ref, west0_ref = east0_ref.at[at0], west0_ref.at[at0]
    to_east0_ref = to_east0_ref.at[to_east0_ref.shape[0] - 1]
    to_west0_ref = to_west0_ref.at[to_west0_ref.shape[0] - 1]
    cell, width = east0_ref.shape
    tokens = 4 * cell
    if make:
        same_ref = rest[-1]
        windows = ids_ref.shape[0] // WIN_LAT
        for i in range(windows):
            codes = window_codes(ids_ref, i, cell)
            same_ref[i] = dot_t(
                codes, jnp.concatenate([codes] * (GROUP * heads // width), axis=0)
            ).astype(BF16)
    else:
        same_ref = ids_ref
        windows = same_ref.shape[0]

    def cells(i, e, w, e0, w0):
        last = i == windows - 1
        return [
            e.at[2 * i],
            e0 if last else e.at[2 * i + 1],
            w.at[2 * i],
            w0 if last else w.at[2 * i + 1],
        ]

    x = jnp.concatenate(
        [
            ref[...].astype(F32)
            for i in range(windows)
            for ref in cells(i, east_ref, west_ref, east0_ref, west0_ref)
        ],
        axis=0,
    ).astype(BF16)
    triple = dot(x, qkv_ref[...]).astype(BF16)
    scale_row = scale_lanes(scale_ref, 1, width, heads)
    sames = [same_ref[i] for i in range(windows)]
    results = attend(
        [triple[i * tokens : (i + 1) * tokens] for i in range(windows)], scale_row, sames, heads
    )
    for i, result in enumerate(results):
        att = result.astype(F32)
        for n, ref in enumerate(cells(i, to_east_ref, to_west_ref, to_east0_ref, to_west0_ref)):
            ref[...] = att[n * cell : (n + 1) * cell, :].astype(BF16)


def last_kernel(halves, at0s, before, waits, *refs):
    refs = list(refs)
    jobs = [refs[3 * n : 3 * n + 3] for n in range(len(halves))]
    refs = refs[3 * len(halves) :]
    gain_ref, bias_ref, out_ref, up_ref, down_ref = refs[:5]
    priors, refs = refs[5 : 5 + len(before)], refs[5 + len(before) + waits :]
    final = len(before) > 0
    _, bands, cell, width = jobs[0][0].shape
    line = cell // CELL_LAT
    copies = []
    if final:
        mixed_ref, *y_refs, sems = refs
        columns = [pl.ds(half * CELL_LON, CELL_LON) for half in range(2)]
        for n, (prior, (sample, half)) in enumerate(zip(priors, before)):
            copies.append(
                pltpu.make_async_copy(prior, mixed_ref.at[sample, :, columns[half]], sems.at[n])
            )
            copies[-1].start()
    else:
        y_refs = refs
    pieces, rows = [], []
    for (sample, half), at0, (first_ref, kept, kept0) in zip(halves, at0s, jobs):
        pieces.append(kept0[at0].astype(F32))
        pieces.extend(kept[r].astype(F32) for r in range(bands - 1))
        rows.append(first_ref[half].reshape(bands * cell, width))
    attended = jnp.concatenate(pieces, axis=0).astype(BF16)
    x = jnp.concatenate(rows, axis=0)
    after, mlp = feed_rows(x, attended, out_ref, up_ref, down_ref, gain_ref, bias_ref, 1)
    for n, ((sample, half), y_ref) in enumerate(zip(halves, y_refs)):
        for band in range(bands):
            at = (n * bands + band) * cell
            y = after[at : at + cell] + norm_rows(
                mlp[at : at + cell], gain_ref[1, 1:2], bias_ref[1, 1:2]
            )
            part = pl.ds(band * CELL_LAT, CELL_LAT)
            y_ref[part] = y.reshape(CELL_LAT, CELL_LON, line // CELL_LON, width)
            if final:
                copies.append(
                    pltpu.make_async_copy(
                        y_ref.at[part],
                        mixed_ref.at[sample, part, columns[half]],
                        sems.at[len(copies)],
                    )
                )
                copies[-1].start()
    for c in copies:
        c.wait()


ANY = pl.BlockSpec(memory_space=pl.ANY)
HBM = pl.BlockSpec(memory_space=pltpu.HBM)
SMEM = pl.BlockSpec(memory_space=pltpu.SMEM)
VMEM = pl.BlockSpec(memory_space=pltpu.VMEM)


def params(limit):
    return pltpu.CompilerParams(vmem_limit_bytes=limit << 20)


def in_hbm(array):
    return pltpu.with_memory_space_constraint(array, pltpu.HBM)


def first_layer(grid, sample, held, x, heads, more=(), carried=(), after=()):
    samples, rows, cols, levels, width = grid.shape
    load = sample == 0
    has_next = sample + 1 < samples
    bands = rows // CELL_LAT
    cell = levels * CELL_LAT * CELL_LON
    kept = jax.ShapeDtypeStruct((bands - 1, cell, width), BF16)
    kept0 = jax.ShapeDtypeStruct((1 + len(carried) // 2, cell, width), BF16)
    outs = [jax.ShapeDtypeStruct((2, bands, cell, width), F32), kept, kept, kept0, kept0]
    if has_next:
        outs.append(pltpu.VMEM(grid.shape[1:], F32))
    scratch = [
        pltpu.VMEM((2, bands * cell, width), F32),
        pltpu.VMEM((2, bands * cell, 3 * width), BF16),
        pltpu.VMEM((2, bands * cell, width), BF16),
    ]
    if has_next:
        scratch.append(pltpu.SemaphoreType.DMA((1,)))
    if load:
        held = [in_hbm(h) for h in held]
        outs += [pltpu.VMEM(h.shape, h.dtype) for h in held[:3]]
        outs += [pltpu.VMEM(h.shape[1:], h.dtype) for h in held[3:]]
        scratch = [pltpu.VMEM(grid.shape[1:], F32)] + scratch
    if len(more) > 0:
        more = [in_hbm(m) for m in more]
        outs += [pltpu.VMEM(m.shape[1:], m.dtype) for m in more]
        scratch.append(pltpu.SemaphoreType.DMA((4,)))
    if load:
        scratch += [pltpu.SemaphoreType.DMA((2,)), pltpu.SemaphoreType.DMA((7,))]
    ins = [] if load else [x]
    return pl.pallas_call(
        functools.partial(first_kernel, heads, sample, has_next, len(more) > 0, len(carried), len(after)),
        in_specs=[HBM] + [HBM if load else VMEM] * 7 + [VMEM] * len(ins) + [HBM] * len(more) + [VMEM] * len(carried) + [ANY] * len(after),
        out_specs=[VMEM] * len(outs),
        out_shape=outs,
        scratch_shapes=scratch,
        compiler_params=params(16),
        cost_estimate=pl.CostEstimate(flops=int(8e9*COST), bytes_accessed=int(10e6*COST), transcendentals=0),
        name="first_layer",
    )(in_hbm(grid), *held, *ins, *more, *carried, *after)


def shifted_attention(east, west, east0, west0, at0, ids, scale, qkv, heads, make, carried=(), after=()):
    args = (east, west, east0, west0)
    cell, width = east.shape[1:]
    kept = jax.ShapeDtypeStruct(east.shape, BF16)
    kept0 = jax.ShapeDtypeStruct((1 + len(carried) // 2, cell, width), BF16)
    outs = [kept, kept, kept0, kept0]
    if make:
        tokens = 4 * cell
        keys = tokens * (GROUP * heads // width)
        outs.append(pltpu.VMEM((ids.shape[0] // WIN_LAT, tokens, keys), BF16))
    return pl.pallas_call(
        functools.partial(shifted_kernel, heads, make, at0, len(carried), len(after)),
        in_specs=[VMEM] * 4 + [SMEM if make else VMEM, VMEM, VMEM] + [VMEM] * len(carried) + [ANY] * len(after),
        out_specs=[VMEM] * len(outs),
        out_shape=outs,
        compiler_params=params(16),
        cost_estimate=pl.CostEstimate(flops=int(1e9*COST), bytes_accessed=int(1e6*COST), transcendentals=0),
        name="shifted_attention",
    )(*args, ids, scale, qkv, *carried, *after)


def last_half(halves, jobs, at0s, held, shape, priors=None, after=()):
    _, rows, cols, levels, width = shape
    priors = priors or {}
    final = len(priors) > 0
    y = pltpu.VMEM((rows, CELL_LON, levels, width), F32)
    ys = [y] * len(halves)
    bands = rows // CELL_LAT
    operands = [array for job in jobs for array in job]
    outs = [jax.ShapeDtypeStruct(shape, F32)] if final else ys
    copies = len(priors) + bands * len(halves)
    size = len(halves) / 2 * COST
    return pl.pallas_call(
        functools.partial(last_kernel, tuple(halves), tuple(at0s), tuple(priors), len(after)),
        in_specs=[VMEM] * (len(operands) + 5 + len(priors)) + [ANY] * len(after),
        out_specs=[HBM if final else VMEM] * len(outs),
        out_shape=outs,
        scratch_shapes=ys + [pltpu.SemaphoreType.DMA((copies,))] if final else [],
        compiler_params=params(18),
        cost_estimate=pl.CostEstimate(flops=int(5e9*size), bytes_accessed=int(5e6*size), transcendentals=0),
        name="last_half",
    )(*operands, *held, *priors.values(), *after)


def shifted(x, lat_by, lon_by):
    lat, lon = lax.axis_size("lat"), lax.axis_size("lon")
    pairs = [
        (o * lat + a, (o + lon_by) % lon * lat + (a + lat_by) % lat)
        for o in range(lon)
        for a in range(lat)
    ]
    return lax.ppermute(x, ("lon", "lat"), pairs)


def window_codes(ids_ref, window, cell):
    rows, levels, _ = ids_ref.shape
    lat_total = lax.axis_size("lat") * rows
    start = lax.axis_index("lat") * rows + window * WIN_LAT
    token = lax.broadcasted_iota(jnp.int32, (cell, 128), 0)
    column = lax.rem(token // levels, CELL_LON)
    lane = lax.broadcasted_iota(jnp.int32, (cell, 128), 1)
    codes = []
    for half in range(2):
        ids = jnp.zeros((cell, 128), jnp.int32)
        for c in range(CELL_LON):
            ids = jnp.where(column == c, ids_ref[window * WIN_LAT, 0, half * CELL_LON + c], ids)
        for r in range(2):
            at = start + r * CELL_LAT
            band = jnp.where(at >= lat_total - WIN_LAT, 1, 0) + jnp.where(
                at >= lat_total - CELL_LAT, 1, 0
            )
            codes.append(jnp.where(ids * 3 + band == lane, 1.0, 0.0))
    return jnp.concatenate(codes, axis=0).astype(BF16)


def local(stream, region_ids, qkv, out, up, down, gain, bias, scale):
    samples = stream.shape[0]
    heads = scale.shape[1]
    ids = region_ids.transpose(1, 0, 2)
    grid = stream.transpose(0, 2, 3, 1, 4)
    weights = [qkv, out, up, down]
    held = [scale, gain, bias] + weights
    firsts, halos, backs, same, x = [], [], [], [], None
    place = [max(s, 1) for s in range(samples)] if samples > 1 else [0]
    at0s = [1 if s == 1 else 0 for s in range(samples)]
    sent0, back0 = {}, {}
    for s in range(samples):
        after = [halos[s - 2][1]] if s >= 2 else ()
        more = weights if s == min(1, samples - 1) else ()
        carried = made0 if s == 1 else ()
        made = first_layer(grid, s, held, x, heads, more, carried, after)
        first, east, west, *made0 = made[:5]
        made = made[5:]
        if s + 1 < samples:
            x, made = made[0], made[1:]
        if s == 0:
            held, made = made[:7], made[7:]
        if len(more) > 0:
            later = made
        firsts.append(first)
        if place[s] == s:
            sent0[s] = (shifted(made0[0], -1, 0), shifted(made0[1], -1, -1))
        halos.append((east, shifted(west, 0, -1)))
    for s in range(samples):
        after = [halos[1][1]] if s == 0 and samples > 1 else sent0.get(s + 1, ()) if s > 0 else ()
        keys = same[0] if len(same) > 0 else ids
        carried = made0 if s == 1 else ()
        east, west, *made0 = shifted_attention(
            *halos[s], *sent0[place[s]], at0s[s], keys, held[0], later[0], heads,
            len(same) == 0, carried, after,
        )
        made0, more = made0[:2], made0[2:]
        same.extend(more)
        if place[s] == s:
            back0[s] = (shifted(made0[0], 1, 0), shifted(made0[1], 1, 1))
        backs.append((east, shifted(west, 0, 1)))
    feed = [*held[1:3], *later[1:]]
    groups = [[(s, 0), (s, 1)] for s in range(samples - 1)]
    if len(groups) == 0:
        groups.append([])
    groups[-1].append((samples - 1, 1))
    groups.append([(samples - 1, 0)])
    made, ys = {}, ()
    for n, halves in enumerate(groups):
        jobs = []
        for s, half in halves:
            east0, west0 = back0[place[s]]
            jobs.append((firsts[s], backs[s][1], west0) if half == 0 else (firsts[s], backs[s][0], east0))
        final = n == len(groups) - 1
        ys = last_half(halves, jobs, [at0s[s] for s, _ in halves], feed, grid.shape, made if final else None, () if final else ys[:1])
        made.update(zip(halves, ys))
    return ys[0].transpose(0, 3, 1, 2, 4)


def solution(mesh):
    in_specs = (
        P("ens", None, "lat", "lon", None),
        P("ens", "lat", "lon"),
        P(), P(), P(), P(), P(), P(), P(),
    )
    out_specs = P("ens", None, "lat", "lon", None)
    return jax.shard_map(local, mesh=mesh, in_specs=in_specs, out_specs=out_specs, check_vma=False)
```
